32 devices in a mesh: groups: 2 (over y), field: 4 (over x, core), wave: 4 (over z).
Axes of the slice: x: 2, y: 2, z: 4, core: 2. Of those that a mesh axis runs over, the one named last changes fastest.
Arguments:
- mode_basis: bfloat16 [22, 512, 512], P(None, 'wave'), may hold values from -6 to 6
- coef_table: bfloat16 [4096, 22], replicated, may hold values from -1.5 to 1.5
- table_index: int32 [64], P(('groups', 'field')), parts along dimension 0, may hold values from 0 to 4095
- wave_lengths: float32 [8], P('wave'), may hold values from 0.32 to 1.05
- sed_table: float32 [1024, 8], replicated, may hold values from 0.05 to 1
- template_ids: int32 [64, 8], P(('groups', 'field')), parts along dimension 0, may hold values from 0 to 1023
Outputs:
- mixed: bfloat16 [64, 8, 256, 256], P(('groups', 'field'), None, 'wave'), parts along dimension 0
The draws below stay inside these ranges and needn't reach their ends.
There are 2 independent parts, one for each index of `groups`. The reference program is written for one: setup_inputs(seed, part) draws one part's arguments, and reference() takes and returns one part's arrays. A program takes and returns all parts, laid end to end along the dimension named above; an argument that names none is the same for every part. Nothing has to cross between parts.
All inputs are finite; a program needn't handle non-finite values.
Results may differ from the reference program's by a relative error of at most 0.0065.
Values may be sent and summed in bfloat16 or wider, within the bound.
A program may use at most 128 MiB of HBM per device.

```python
import math
import jax
import jax.numpy as jnp
from jax import lax

PUP = 512
PIX = 256
K = 22
NTAB = 4096
NSED = 1024
J = 8
F = 32
W = 8


def with_ends(values, rng, least, largest):
    longest = values.shape.index(max(values.shape))
    spots = []
    for shift in (0, 1):
        where = [jax.random.randint(jax.random.fold_in(rng, axis), (), 0, length) for axis, length in enumerate(values.shape)]
        where[longest] = (where[longest] + shift) % values.shape[longest]
        spots.append(tuple(where))
    return values.at[spots[0]].set(least).at[spots[1]].set(largest)


def levels(key, extent, pieces, least, largest):
    level = 1.0
    for position, shards_of in pieces:
        steps = jax.random.uniform(jax.random.fold_in(jax.random.fold_in(key, 6), position), (shards_of,), jnp.float32, least / len(pieces), largest / len(pieces))
        level = level * jnp.repeat(jnp.exp(steps), extent[position] // shards_of).reshape((-1,) + (1,) * (len(extent) - 1 - position))
    return level


def gaussian(own_key, shape, deviation, reach, shards=(), held_as=jnp.bfloat16):
    array = jax.random.normal(own_key, shape, jnp.float32) * deviation
    if len(shards) > 0:
        array = levels(own_key, shape, shards, -0.22, 0.18) * array
    return jnp.clip(array, min=-reach, max=reach).astype(held_as)


def setup_inputs(seed: int = 0, part: int = 0) -> dict:
    key_list = jax.random.split(jax.random.key(seed), 7)
    part_keys = jax.random.split(jax.random.fold_in(key_list[6], part), 7)
    mode_basis = gaussian(key_list[0], (K, PUP, PUP), 1.0, 6.0, ((1, 4),))
    coef_table = gaussian(key_list[1], (NTAB, K), 0.25, 1.5)
    table_index = with_ends(jax.random.randint(part_keys[2], (F,), 0, NTAB), jax.random.fold_in(part_keys[2], 1), 0, NTAB - 1).astype(jnp.int32)
    wave_lengths = jnp.clip(jnp.exp(math.log(1.05) - 1.1882244 * jax.random.uniform(key_list[3], (W,), jnp.float32) ** levels(key_list[3], (W,), ((0, 4),), -0.2, 0.2)), 0.32, 1.05)
    sed_table = jnp.clip(jnp.exp(jax.random.uniform(key_list[4], (NSED, W), jnp.float32, math.log(0.05), math.log(1.0))), 0.05, 1.0)
    template_ids = with_ends(jax.random.randint(part_keys[5], (F, J), 0, NSED), jax.random.fold_in(part_keys[5], 1), 0, NSED - 1).astype(jnp.int32)
    return dict(mode_basis=mode_basis, coef_table=coef_table, table_index=table_index, wave_lengths=wave_lengths, sed_table=sed_table, template_ids=template_ids)


TWO_PI = 2.0 * math.pi
SAMPLING = 0.25
EPSILON = 1e-6


def transform_table(wave_lengths, pixels, pupil_side):
    pixel_offset = jnp.arange(pixels, dtype=jnp.int32) - pixels // 2
    pupil_offset = 2 * jnp.arange(pupil_side, dtype=jnp.int32) - pupil_side + 1
    products = (pixel_offset[:, None] * pupil_offset[None, :]).astype(jnp.float32)
    factor = (TWO_PI * SAMPLING / (2.0 * pupil_side)) / wave_lengths
    angles = products[None, :, :] * factor[:, None, None]
    cosine = jnp.cos(angles)
    sine_part = jnp.sin(angles)
    upper_half = jnp.concatenate([cosine, sine_part], axis=2)
    lower_half = jnp.concatenate([-sine_part, cosine], axis=2)
    return jnp.concatenate([upper_half, lower_half], axis=1).astype(jnp.bfloat16)


def aperture_rows(row_start, row_count, pupil_side):
    row_pos = 2 * (row_start + jnp.arange(row_count, dtype=jnp.int32)) - pupil_side + 1
    col_pos = 2 * jnp.arange(pupil_side, dtype=jnp.int32) - pupil_side + 1
    radius_sq = row_pos[:, None] * row_pos[:, None] + col_pos[None, :] * col_pos[None, :]
    inner_edge = (61 * pupil_side) // 100
    inside = (radius_sq <= pupil_side * pupil_side) & (radius_sq >= inner_edge * inner_edge)
    return inside.astype(jnp.float32)


def pupil_section(path_rows, wave_lengths, kernel_table):
    row_count = path_rows.shape[1]
    pupil_side = path_rows.shape[2]
    opening = aperture_rows(0, row_count, pupil_side)
    phase_map = path_rows[:, None, :, :] * (TWO_PI / wave_lengths)[None, :, None, None]
    field_real = opening * jnp.cos(phase_map)
    field_imag = opening * jnp.sin(phase_map)
    pupil_field = jnp.concatenate([field_real, field_imag], axis=3).astype(jnp.bfloat16)
    first_pass = jnp.einsum("flxy,luy->flxu", pupil_field.astype(jnp.float32), kernel_table.astype(jnp.float32))
    return first_pass.astype(jnp.bfloat16)


def finish_section(first_pass, kernel_table):
    pixels = first_pass.shape[3] // 2
    stacked = jnp.concatenate([first_pass[..., :pixels], first_pass[..., pixels:]], axis=2)
    image_field = jnp.einsum("lux,flxv->fluv", kernel_table.astype(jnp.float32), stacked.astype(jnp.float32))
    intensity = image_field[:, :, :pixels] * image_field[:, :, :pixels] + image_field[:, :, pixels:] * image_field[:, :, pixels:]
    mean_level = jnp.mean(intensity, axis=(2, 3), keepdims=True)
    return (intensity / (mean_level + EPSILON)).astype(jnp.bfloat16)


def reference(mode_basis, coef_table, table_index, wave_lengths, sed_table, template_ids):
    kernel_table = transform_table(wave_lengths, PIX, PUP)
    flat_basis = mode_basis.reshape(K, PUP * PUP)

    def one_position(inputs):
        index_value, id_row = inputs
        coeffs = coef_table[index_value]
        path_diff = jnp.dot(coeffs[None, :], flat_basis, preferred_element_type=jnp.float32).reshape(1, PUP, PUP)
        first_pass = pupil_section(path_diff, wave_lengths, kernel_table)
        spectra = finish_section(first_pass, kernel_table)
        raw_weights = sed_table[id_row]
        weights = (raw_weights / jnp.sum(raw_weights, axis=1, keepdims=True)).astype(jnp.bfloat16)
        mixed = jnp.einsum("jl,lrp->jrp", weights.astype(jnp.float32), spectra[0].astype(jnp.float32))
        return mixed.astype(jnp.bfloat16)

    return lax.map(one_position, (table_index, template_ids))
```

```python
import functools

import jax
import jax.numpy as jnp
import numpy as np
from jax import lax
from jax.experimental import pallas as pl
from jax.experimental.pallas import tpu as pltpu
from jax.sharding import PartitionSpec as P

PUP = 512
PIX = 256
EPSILON = 1e-06
GROUP = 16
LANES = 128
CHUNKS = 2
ROUNDER = 12582912.0

SIN = (4.442879676818848, -7.307816505432129, 3.5977742671966553, -0.7911993861198425)
COS = (1.4142135381698608, -6.978850841522217, 5.739460468292236, -1.883557915687561, 0.3106880187988281)
SHORT_SIN = (4.440917015075684, -7.256804466247559, 3.229630470275879)
SHORT_COS = (1.414183259010315, -6.976953506469727, 5.709674835205078, -1.7155721187591553)


def horner(coefficients, s):
    value = coefficients[-1]
    for c in coefficients[-2::-1]:
        value = c + s * value
    return value


def turns_sincos(turns, sine=SIN, cosine=COS):
    nearest = (turns + ROUNDER) - ROUNDER
    r = turns - nearest
    s = r * r
    a = r * horner(sine, s)
    b = horner(cosine, s)
    return 1.0 - a * a, a * b


def packed_tiles(slabs, rows):
    pos = 2 * np.arange(PUP) - PUP + 1
    radius = pos[:, None] ** 2 + pos[None, :] ** 2
    inside = (radius <= PUP * PUP) & (radius >= (61 * PUP // 100) ** 2)
    columns = PUP // LANES
    half = LANES // 2
    result = []
    for slab in range(slabs):
        tiles = []
        for group in range(rows // GROUP):
            first = slab * rows + group * GROUP
            need = inside[first : first + GROUP].any(axis=0).reshape(columns, LANES)
            low, high = need[:, :half].any(axis=1), need[:, half:].any(axis=1)
            lows = [c for c in range(columns) if low[c] and not high[c]]
            highs = [c for c in range(columns) if high[c] and not low[c]]
            pairs = list(zip(lows, highs))
            for c in range(columns):
                if low[c] and high[c]:
                    tiles.append((group, (c,)))
            tiles += [(group, pair) for pair in pairs]
            tiles += [(group, (c,)) for c in lows[len(pairs) :] + highs[len(pairs) :]]
        result.append(tuple(tiles))
    return result


def hop(order, slabs):
    odd = order % 2
    return odd * ((order + 1) // 2) + (1 - odd) * (slabs - order // 2)


def psf_kernel(
    sizes, waves, fields, share, mix_ref, weight_ref, length_ref, basis_ref, out_ref,
    held, whole, inverse, path, image, tables, efield0, efield1, opening, power, total, arrived,
    local_sem, wl_send, wl_recv, send1, recv1, send2, recv2, send3, recv3, sum_send, sum_recv,
):
    slabs, field_parts, group_parts = sizes
    count, rows, _ = basis_ref.shape
    upix = PIX // slabs
    own_waves = waves // slabs
    x_parts = field_parts // 2
    chips = x_parts * group_parts
    templates = out_ref.shape[1]
    layout = packed_tiles(slabs, rows)
    kept_tables = tables.shape[0] == waves

    me = lax.axis_index("wave")
    part = lax.axis_index("field")
    core = part % 2
    chip = lax.axis_index("groups") * x_parts + part // 2
    first_pix = me * upix

    def wave_peer(shift):
        return {"wave": (me + shift) % slabs}

    def chip_device(other):
        return {"groups": other // x_parts, "field": (other % x_parts) * 2 + core}

    sibling = {"field": part + 1 - 2 * core}

    def remote(src, dst, send, recv, device):
        return pltpu.make_async_remote_copy(
            src_ref=src, dst_ref=dst, send_sem=send, recv_sem=recv,
            device_id=device, device_id_type=pl.DeviceIdType.MESH,
        )

    def from_slab(order):
        return (me + 2 * slabs - hop(order, slabs)) % slabs

    def block(slab, of_core, chunk, of_chip, pieces=1):
        first = ((of_core * CHUNKS + chunk) * chips + of_chip) * share
        return whole.at[slab, pl.ds(first, pieces * share)]

    def first_copy(order, chunk):
        ref = block(me, core, chunk, chip)
        at = (order - 1, chunk)
        return remote(ref, ref, send1.at[at], recv1.at[at], wave_peer(hop(order, slabs)))

    def first_landed(order, chunk):
        ref = block(from_slab(order), core, chunk, chip)
        at = (order - 1, chunk)
        return remote(ref, ref, send1.at[at], recv1.at[at], wave_peer(hop(order, slabs)))

    relay = x_parts == 2 and group_parts == 2
    chip_x, chip_y = chip % x_parts, chip // x_parts
    flip_x, flip_y = 1 - 2 * chip_x, 1 - 2 * chip_y
    first_chip = (chip_y + core * flip_y) * x_parts + chip_x + (1 - core) * flip_x
    second_chip = (chip_y + (1 - core) * flip_y) * x_parts + chip_x + core * flip_x

    def plane_copy(order, chunk, shift):
        at = (order - 1, chunk, shift - 1)
        slab = from_slab(order)
        if relay:
            ref = block(slab, core, chunk, first_chip if shift == 3 else chip)
            device = chip_device(first_chip if shift == 1 else second_chip)
        else:
            ref = block(slab, core, chunk, chip)
            device = chip_device((chip + shift) % chips)
        return remote(ref, ref, send2.at[at], recv2.at[at], device)

    def plane_landed(order, chunk, shift):
        at = (order - 1, chunk, shift - 1)
        if relay:
            sender = (first_chip, second_chip, chips - 1 - chip)[shift - 1]
        else:
            sender = (chip + chips - shift) % chips
        ref = block(from_slab(order), core, chunk, sender)
        return remote(ref, ref, send2.at[at], recv2.at[at], chip_device((chip + shift) % chips))

    def core_copy(order, chunk, which):
        ref = block(from_slab(order), which, chunk, 0, chips)
        at = (order - 1, chunk)
        return remote(ref, ref, send3.at[at], recv3.at[at], sibling)

    def length_copy(shift, sender):
        ref = inverse.at[pl.ds(sender * own_waves, own_waves)]
        return remote(ref, ref, wl_send.at[shift - 1], wl_recv.at[shift - 1], wave_peer(shift))

    barrier = pltpu.get_barrier_semaphore()
    peers = [wave_peer(d) for d in range(1, slabs)] + [chip_device((chip + e) % chips) for e in range(1, chips)] + [sibling]
    for peer in peers:
        pl.semaphore_signal(barrier, inc=1, device_id=peer, device_id_type=pl.DeviceIdType.MESH)
    bring = pltpu.make_async_copy(basis_ref, held, local_sem)
    bring.start()
    for i in range(own_waves):
        inverse[me * own_waves + i] = 1.0 / jnp.full(inverse.shape[1:], length_ref[i], jnp.float32)

    def clear(f, carry):
        for l in range(waves):
            image[l, pl.ds(f * upix, upix), :] = jnp.zeros((upix, 2 * PUP), jnp.float32)
        return carry

    lax.fori_loop(0, fields, clear, 0)
    bring.wait()

    low_lanes = (lax.broadcasted_iota(jnp.int32, (GROUP, LANES), 1) < LANES // 2).astype(jnp.float32)
    low_lanes, high_lanes = low_lanes.astype(jnp.bfloat16), (1.0 - low_lanes).astype(jnp.bfloat16)

    def pack(tiles, k, carry):
        for t, (group, columns) in enumerate(tiles):
            r = group * GROUP
            parts = [held[k, r : r + GROUP, c * LANES : (c + 1) * LANES] for c in columns]
            value = parts[0]
            if len(parts) == 2:
                value = parts[0] * low_lanes + parts[1] * high_lanes
            whole[me, t * count + k] = value
        return carry

    for slab, tiles in enumerate(layout):

        @pl.when(me == slab)
        def _():
            lax.fori_loop(0, count, functools.partial(pack, tiles), 0)

    pl.semaphore_wait(barrier, len(peers))
    for c in range(CHUNKS):
        first_copy(1, c).start()
    for d in range(1, slabs):
        length_copy(d, me).start()
    for d in range(1, slabs):
        length_copy(d, (me + slabs - d) % slabs).wait_recv()

    def second_table(wave, slot):
        scale = inverse[wave][:1, :PIX] * (0.25 / (2.0 * PUP))
        step = 64
        for r in range(0, PUP, step):
            ys = 2 * (r + lax.broadcasted_iota(jnp.int32, (step, PIX), 0)) - PUP + 1
            vs = lax.broadcasted_iota(jnp.int32, (step, PIX), 1) - PIX // 2
            cosine, sine = turns_sincos((ys * vs).astype(jnp.float32) * scale)
            cosine = cosine.astype(jnp.bfloat16)
            tables[slot, r : r + step, :PIX] = cosine
            tables[slot, r : r + step, PIX:] = (-sine).astype(jnp.bfloat16)
            tables[slot, PUP + r : PUP + r + step, :PIX] = sine.astype(jnp.bfloat16)
            tables[slot, PUP + r : PUP + r + step, PIX:] = cosine

    def at_eighth(order, eighths):
        return (order - 1) * waves + eighths * waves // 8

    def step_body(step, carry):
        order = step // waves
        wave = step % waves
        slab = from_slab(order)
        first_row = slab * rows

        if kept_tables:

            @pl.when(step == waves)
            def _():
                def make(l, c):
                    second_table(l, l)
                    return c

                lax.fori_loop(0, waves, make, 0)

        for o in range(1, slabs):
            for c in range(CHUNKS):

                @pl.when(step == at_eighth(o, 2 + 2 * c))
                def _():
                    first_landed(o, c).wait_recv()
                    for e in range(1, 3 if relay else chips):
                        plane_copy(o, c, e).start()
                    if o + 1 < slabs:
                        first_copy(o + 1, c).start()

                if relay:

                    @pl.when(step == at_eighth(o, 4 + 2 * c))
                    def _():
                        plane_landed(o, c, 1).wait_recv()
                        plane_copy(o, c, 3).start()

                @pl.when(step == at_eighth(o, 6 + 2 * c))
                def _():
                    for e in range(2 if relay else 1, chips):
                        plane_landed(o, c, e).wait_recv()
                    core_copy(o, c, core).start()

            @pl.when(step == o * waves)
            def _():
                for c in range(CHUNKS):
                    core_copy(o, c, 1 - core).wait_recv()

        @pl.when(wave == 0)
        def _():
            def paths(i, c):
                pair = [whole[slab, pl.ds((2 * i + b) * count, count)].reshape(count * GROUP, LANES) for b in range(2)]
                diff = jnp.dot(mix_ref[...], jnp.concatenate(pair, axis=1), preferred_element_type=jnp.float32)
                for b in range(2):
                    path[:, 2 * i + b] = diff[:, b * LANES : (b + 1) * LANES].reshape(fields, GROUP, LANES)
                return c

            def openings(g, c):
                r = pl.multiple_of(g * GROUP, GROUP)
                x = 2 * (first_row + r + lax.broadcasted_iota(jnp.int32, (GROUP, PUP), 0)) - PUP + 1
                y = 2 * lax.broadcasted_iota(jnp.int32, (GROUP, PUP), 1) - PUP + 1
                radius = x * x + y * y
                inner = 61 * PUP // 100
                inside = (radius <= PUP * PUP) & (radius >= inner * inner)
                opening[pl.ds(r, GROUP), :] = inside.astype(jnp.float32).astype(jnp.bfloat16)
                return c

            pairs = 0
            for s, tiles in enumerate(layout):
                pairs = jnp.where(slab == s, (len(tiles) + 1) // 2, pairs)
            lax.fori_loop(0, pairs, paths, 0)
            lax.fori_loop(0, rows // GROUP, openings, 0)
            for field in (efield0, efield1):
                field[...] = jnp.zeros_like(field)

        inv = inverse[wave]
        lane = lax.broadcasted_iota(jnp.int32, (upix, 2 * rows), 1)
        real = lane < rows
        xs = 2 * (first_row + jnp.where(real, lane, lane - rows)) - PUP + 1
        us = first_pix + lax.broadcasted_iota(jnp.int32, (upix, 2 * rows), 0) - PIX // 2
        scale = inv[:1, : 2 * rows] * (0.25 / (2.0 * PUP))
        cosine, sine = turns_sincos((us * xs).astype(jnp.float32) * scale)
        kernel = jnp.concatenate(
            [jnp.where(real, cosine, sine), jnp.where(real, -sine, cosine)], axis=0
        ).astype(jnp.bfloat16)
        tile = jnp.concatenate([inv[:, :LANES], inv[:, :LANES]], axis=0)

        def accumulate(f):
            field = (efield0, efield1)[f % 2]
            part_sum = jnp.dot(kernel, field[...], preferred_element_type=jnp.float32)
            here = pl.ds(f * upix, upix)
            image[wave, here, :PUP] += part_sum[:upix]
            image[wave, here, PUP:] += part_sum[upix:]

        def units(tiles):
            for f in range(fields):
                field = (efield0, efield1)[f % 2]
                for t, (group, columns) in enumerate(tiles):
                    r = group * GROUP
                    cosine, sine = turns_sincos(path[f, t] * tile, SHORT_SIN, SHORT_COS)
                    cosine, sine = cosine.astype(jnp.bfloat16), sine.astype(jnp.bfloat16)
                    for c in columns:
                        lanes = slice(c * LANES, (c + 1) * LANES)
                        hole = opening[r : r + GROUP, lanes]
                        field[r : r + GROUP, lanes] = cosine * hole
                        field[rows + r : rows + r + GROUP, lanes] = sine * hole
                if f > 0:
                    accumulate(f - 1)
            accumulate(fields - 1)

        for s, tiles in enumerate(layout):
            pl.when(slab == s)(functools.partial(units, tiles))

        return carry

    lax.fori_loop(0, slabs * waves, step_body, 0)

    def finish(wave, carry):
        if not kept_tables:
            second_table(wave, 0)
        slot = wave if kept_tables else 0
        half = fields * upix // 2
        for h in range(2):
            field = jnp.dot(
                image[wave, h * half : (h + 1) * half, :].astype(jnp.bfloat16),
                tables[slot],
                preferred_element_type=jnp.float32,
            )
            re, im = field[:, :PIX], field[:, PIX:]
            bright = re * re + im * im
            power[wave, h * half : (h + 1) * half, :] = bright
            sums = jnp.sum(jnp.sum(bright.reshape(fields // 2, upix, PIX), axis=1), axis=1, keepdims=True)
            total[wave, h * (fields // 2) : (h + 1) * (fields // 2), :] = jnp.broadcast_to(
                sums, (fields // 2, PIX)
            )
        return carry

    lax.fori_loop(0, waves, finish, 0)

    def sum_copy(shift):
        return remote(
            total, arrived.at[shift - 1], sum_send.at[shift - 1], sum_recv.at[shift - 1], wave_peer(shift)
        )

    for d in range(1, slabs):
        sum_copy(d).start()
    for d in range(1, slabs):
        sum_copy(d).wait()
    everything = total[...]
    for d in range(1, slabs):
        everything = everything + arrived[d - 1]
    total[...] = 1.0 / (everything * (1.0 / (PIX * PIX)) + EPSILON)

    step = 16

    def mix_fields(f, carry):
        for r in range(0, upix, step):
            sums = [None] * templates
            for l in range(waves):
                level = total[l, pl.ds(f, 1), :]
                bright = power[l, pl.ds(pl.multiple_of(f * upix, step) + r, step), :]
                spectrum = (bright * level).astype(jnp.bfloat16).astype(jnp.float32)
                for j in range(templates):
                    term = spectrum * weight_ref[(f * templates + j) * waves + l]
                    sums[j] = term if l == 0 else sums[j] + term
            for j in range(templates):
                out_ref[f, j, r : r + step, :] = sums[j].astype(jnp.bfloat16)
        return carry

    lax.fori_loop(0, fields, mix_fields, 0)

    for d in range(1, slabs):
        length_copy(d, me).wait_send()
    for o in range(1, slabs):
        for c in range(CHUNKS):
            first_copy(o, c).wait_send()
            for e in range(1, chips):
                plane_copy(o, c, e).wait_send()
            core_copy(o, c, core).wait_send()


def local(sizes, waves, mode_basis, coef_table, table_index, wave_lengths, sed_table, template_ids):
    slabs, field_parts, group_parts = sizes
    count, rows, _ = mode_basis.shape
    fields, templates = template_ids.shape
    upix = PIX // slabs
    chips = field_parts * group_parts // 2
    tiles = max(len(t) for t in packed_tiles(slabs, rows))
    share = -(-tiles * count // (2 * CHUNKS * chips))
    even = tiles + tiles % 2
    units = max(share * 2 * CHUNKS * chips, even * count)

    coeffs = jnp.take(coef_table, table_index, axis=0, mode="clip")
    same = jnp.eye(GROUP, dtype=jnp.bfloat16)
    mix = (coeffs[:, None, :, None] * same[None, :, None, :]).reshape(fields * GROUP, -1)
    raw = jnp.take(sed_table, template_ids, axis=0, mode="clip")
    weights = (raw / jnp.sum(raw, axis=2, keepdims=True)).astype(jnp.bfloat16).astype(jnp.float32)
    hops = slabs - 1
    dma = pltpu.SemaphoreType.DMA

    return pl.pallas_call(
        functools.partial(psf_kernel, sizes, waves, fields, share),
        in_specs=[
            pl.BlockSpec(memory_space=pltpu.VMEM),
            pl.BlockSpec(memory_space=pltpu.SMEM),
            pl.BlockSpec(memory_space=pltpu.SMEM),
            pl.BlockSpec(memory_space=pl.ANY),
        ],
        out_specs=pl.BlockSpec(memory_space=pltpu.VMEM),
        out_shape=jax.ShapeDtypeStruct((fields, templates, upix, PIX), jnp.bfloat16),
        scratch_shapes=[
            pltpu.VMEM((count, rows, PUP), jnp.bfloat16),
            pltpu.VMEM((slabs, units, GROUP, LANES), jnp.bfloat16),
            pltpu.VMEM((waves, 8, max(2 * rows, PIX)), jnp.float32),
            pltpu.VMEM((fields, even, GROUP, LANES), jnp.float32),
            pltpu.VMEM((waves, fields * upix, 2 * PUP), jnp.float32),
            pltpu.VMEM((waves if waves <= 8 else 1, 2 * PUP, 2 * PIX), jnp.bfloat16),
            pltpu.VMEM((2 * rows, PUP), jnp.bfloat16),
            pltpu.VMEM((2 * rows, PUP), jnp.bfloat16),
            pltpu.VMEM((rows, PUP), jnp.bfloat16),
            pltpu.VMEM((waves, fields * upix, PIX), jnp.float32),
            pltpu.VMEM((waves, fields, PIX), jnp.float32),
            pltpu.VMEM((hops, waves, fields, PIX), jnp.float32),
            dma,
            dma((hops,)),
            dma((hops,)),
            dma((hops, CHUNKS)),
            dma((hops, CHUNKS)),
            dma((hops, CHUNKS, chips - 1)),
            dma((hops, CHUNKS, chips - 1)),
            dma((hops, CHUNKS)),
            dma((hops, CHUNKS)),
            dma((hops,)),
            dma((hops,)),
        ],
        compiler_params=pltpu.CompilerParams(
            vmem_limit_bytes=60 * 2**20, collective_id=0, has_side_effects=True
        ),
    )(mix, weights.reshape(-1), wave_lengths, mode_basis)


def solution(mesh):
    sizes = (mesh.shape["wave"], mesh.shape["field"], mesh.shape["groups"])


    def whole_program(*args):
        return sharded(mesh, functools.partial(local, sizes, args[3].shape[0]))(*args)

    return whole_program


def sharded(mesh, body):
    return jax.shard_map(
        body,
        mesh=mesh,
        in_specs=(
            P(None, "wave", None),
            P(),
            P(("groups", "field")),
            P("wave"),
            P(),
            P(("groups", "field"), None),
        ),
        out_specs=P(("groups", "field"), None, "wave", None),
        check_vma=False,
    )
```

```python
import functools

import jax
import jax.numpy as jnp
import numpy as np
from jax import lax
from jax.experimental import pallas as pl
from jax.experimental.pallas import tpu as pltpu
from jax.sharding import PartitionSpec as P

PUP = 512
PIX = 256
EPSILON = 1e-06
GROUP = 16
LANES = 128
CHUNKS = 2
ROUNDER = 12582912.0

SIN = (4.442879676818848, -7.307816505432129, 3.5977742671966553, -0.7911993861198425)
COS = (1.4142135381698608, -6.978850841522217, 5.739460468292236, -1.883557915687561, 0.3106880187988281)
SHORT_SIN = (4.440917015075684, -7.256804466247559, 3.229630470275879)
SHORT_COS = (1.414183259010315, -6.976953506469727, 5.709674835205078, -1.7155721187591553)


def horner(coefficients, s):
    value = coefficients[-1]
    for c in coefficients[-2::-1]:
        value = c + s * value
    return value


def turns_sincos(turns, sine=SIN, cosine=COS):
    nearest = (turns + ROUNDER) - ROUNDER
    r = turns - nearest
    s = r * r
    a = r * horner(sine, s)
    b = horner(cosine, s)
    return 1.0 - a * a, a * b


def packed_tiles(slabs, rows):
    pos = 2 * np.arange(PUP) - PUP + 1
    radius = pos[:, None] ** 2 + pos[None, :] ** 2
    inside = (radius <= PUP * PUP) & (radius >= (61 * PUP // 100) ** 2)
    columns = PUP // LANES
    half = LANES // 2
    result = []
    for slab in range(slabs):
        tiles = []
        for group in range(rows // GROUP):
            first = slab * rows + group * GROUP
            need = inside[first : first + GROUP].any(axis=0).reshape(columns, LANES)
            low, high = need[:, :half].any(axis=1), need[:, half:].any(axis=1)
            lows = [c for c in range(columns) if low[c] and not high[c]]
            highs = [c for c in range(columns) if high[c] and not low[c]]
            pairs = list(zip(lows, highs))
            for c in range(columns):
                if low[c] and high[c]:
                    tiles.append((group, (c,)))
            tiles += [(group, pair) for pair in pairs]
            tiles += [(group, (c,)) for c in lows[len(pairs) :] + highs[len(pairs) :]]
        result.append(tuple(tiles))
    return result


def hop(order, slabs):
    odd = order % 2
    return odd * ((order + 1) // 2) + (1 - odd) * (slabs - order // 2)


def events_of(slabs):
    timed = []
    for order in range(1, slabs):
        for chunk in range(CHUNKS):
            q = (order - 1) * CHUNKS + chunk
            timed += [(3 * q, (1, order, chunk)), (3 * q + 4, (2, order, chunk)), (3 * q + 6.5, (3, order, chunk))]
        timed.append((3 * q + 6.75, (4, order, 0)))
    return [event for _, event in sorted(timed)]


def scheduled_events(slabs, waves):
    plan, pending, reached = {}, [], 0
    for event in events_of(slabs):
        pending.append(event)
        if event[0] == 4:
            start = reached * waves
            for i, early in enumerate(pending):
                step = start + waves * (i + 1) // len(pending)
                if reached == 0:
                    step = 5 * waves // 8 if i == 0 else waves
                plan.setdefault(step if early[0] != 4 else (reached + 1) * waves, []).append(early)
            pending, reached = [], event[1]
    return plan


def psf_kernel(
    sizes, waves, fields, share, mix_ref, weight_ref, length_ref, basis_ref, out_ref,
    held, whole, inverse, path, image, tables, xtables, efield0, efield1, opening, power, total, arrived, staged,
    local_sem, wl_send, wl_recv, send1, recv1, send2, recv2, send3, recv3, sum_send, sum_recv, out_send, out_recv,
):
    slabs, field_parts, group_parts = sizes
    count, rows, _ = basis_ref.shape
    upix = 2 * PIX // slabs
    own_waves = waves // slabs
    pairs = slabs // 2
    x_parts = field_parts // 2
    chips = x_parts * group_parts
    templates = out_ref.shape[1]
    layout = packed_tiles(slabs, rows)
    kept_tables = tables.shape[0] == waves

    me = lax.axis_index("wave")
    part = lax.axis_index("field")
    core = part % 2
    chip = lax.axis_index("groups") * x_parts + part // 2
    side = me % 2
    first_pix = (me // 2) * upix
    partner = {"wave": me + 1 - 2 * side}

    def wave_peer(shift):
        return {"wave": (me + shift) % slabs}

    def chip_device(other):
        return {"groups": other // x_parts, "field": (other % x_parts) * 2 + core}

    sibling = {"field": part + 1 - 2 * core}

    def remote(src, dst, send, recv, device):
        return pltpu.make_async_remote_copy(
            src_ref=src, dst_ref=dst, send_sem=send, recv_sem=recv,
            device_id=device, device_id_type=pl.DeviceIdType.MESH,
        )

    def from_slab(order):
        return (me + 2 * slabs - hop(order, slabs)) % slabs

    def block(slab, of_core, chunk, of_chip, pieces=1):
        first = ((of_core * CHUNKS + chunk) * chips + of_chip) * share
        return whole.at[slab, pl.ds(first, pieces * share)]

    def first_copy(order, chunk):
        ref = block(me, core, chunk, chip)
        at = (order - 1, chunk)
        return remote(ref, ref, send1.at[at], recv1.at[at], wave_peer(hop(order, slabs)))

    def first_landed(order, chunk):
        ref = block(from_slab(order), core, chunk, chip)
        at = (order - 1, chunk)
        return remote(ref, ref, send1.at[at], recv1.at[at], wave_peer(hop(order, slabs)))

    relay = x_parts == 2 and group_parts == 2
    chip_x, chip_y = chip % x_parts, chip // x_parts
    flip_x, flip_y = 1 - 2 * chip_x, 1 - 2 * chip_y
    first_chip = (chip_y + core * flip_y) * x_parts + chip_x + (1 - core) * flip_x
    second_chip = (chip_y + (1 - core) * flip_y) * x_parts + chip_x + core * flip_x

    def plane_copy(order, chunk, shift):
        at = (order - 1, chunk, shift - 1)
        slab = from_slab(order)
        if relay:
            ref = block(slab, core, chunk, first_chip if shift == 3 else chip)
            device = chip_device(first_chip if shift == 1 else second_chip)
        else:
            ref = block(slab, core, chunk, chip)
            device = chip_device((chip + shift) % chips)
        return remote(ref, ref, send2.at[at], recv2.at[at], device)

    def plane_landed(order, chunk, shift):
        at = (order - 1, chunk, shift - 1)
        if relay:
            sender = (first_chip, second_chip, chips - 1 - chip)[shift - 1]
        else:
            sender = (chip + chips - shift) % chips
        ref = block(from_slab(order), core, chunk, sender)
        return remote(ref, ref, send2.at[at], recv2.at[at], chip_device((chip + shift) % chips))

    def core_copy(order, chunk, which):
        ref = block(from_slab(order), which, chunk, 0, chips)
        at = (order - 1, chunk)
        return remote(ref, ref, send3.at[at], recv3.at[at], sibling)

    def length_copy(shift, sender):
        ref = inverse.at[pl.ds(sender * own_waves, own_waves)]
        return remote(ref, ref, wl_send.at[shift - 1], wl_recv.at[shift - 1], wave_peer(shift))

    barrier = pltpu.get_barrier_semaphore()
    peers = [wave_peer(d) for d in range(1, slabs)] + [chip_device((chip + e) % chips) for e in range(1, chips)] + [sibling]
    for peer in peers:
        pl.semaphore_signal(barrier, inc=1, device_id=peer, device_id_type=pl.DeviceIdType.MESH)
    bring = pltpu.make_async_copy(basis_ref, held, local_sem)
    bring.start()
    for i in range(own_waves):
        inverse[me * own_waves + i] = 1.0 / jnp.full(inverse.shape[1:], length_ref[i], jnp.float32)

    def clear(f, carry):
        for l in range(waves):
            image[l, pl.ds(f * upix, upix), :] = jnp.zeros((upix, 2 * PUP), jnp.float32)
        return carry

    lax.fori_loop(0, fields, clear, 0)
    bring.wait()

    low_lanes = (lax.broadcasted_iota(jnp.int32, (GROUP, LANES), 1) < LANES // 2).astype(jnp.float32)
    low_lanes, high_lanes = low_lanes.astype(jnp.bfloat16), (1.0 - low_lanes).astype(jnp.bfloat16)

    def pack(tiles, k, carry):
        for t, (group, columns) in enumerate(tiles):
            r = group * GROUP
            parts = [held[k, r : r + GROUP, c * LANES : (c + 1) * LANES] for c in columns]
            value = parts[0]
            if len(parts) == 2:
                value = parts[0] * low_lanes + parts[1] * high_lanes
            whole[me, t * count + k] = value
        return carry

    for slab, tiles in enumerate(layout):

        @pl.when(me == slab)
        def _():
            lax.fori_loop(0, count, functools.partial(pack, tiles), 0)

    pl.semaphore_wait(barrier, len(peers))
    for c in range(CHUNKS):
        first_copy(1, c).start()
    for d in range(1, slabs):
        length_copy(d, me).start()
    for d in range(1, slabs):
        length_copy(d, (me + slabs - d) % slabs).wait_recv()

    def second_table(wave, slot):
        scale = inverse[wave][:1, :PIX] * (0.25 / (2.0 * PUP))
        step = 64
        for r in range(0, PUP, step):
            ys = 2 * (r + lax.broadcasted_iota(jnp.int32, (step, PIX), 0)) - PUP + 1
            vs = lax.broadcasted_iota(jnp.int32, (step, PIX), 1) - PIX // 2
            cosine, sine = turns_sincos((ys * vs).astype(jnp.float32) * scale)
            cosine = cosine.astype(jnp.bfloat16)
            tables[slot, r : r + step, :PIX] = cosine
            tables[slot, r : r + step, PIX:] = (-sine).astype(jnp.bfloat16)
            tables[slot, PUP + r : PUP + r + step, :PIX] = sine.astype(jnp.bfloat16)
            tables[slot, PUP + r : PUP + r + step, PIX:] = cosine

    def x_table(slab, wave):
        lane = lax.broadcasted_iota(jnp.int32, (upix, 2 * rows), 1)
        real = lane < rows
        xs = 2 * (slab * rows + jnp.where(real, lane, lane - rows)) - PUP + 1
        us = first_pix + lax.broadcasted_iota(jnp.int32, (upix, 2 * rows), 0) - PIX // 2
        scale = inverse[wave][:1, : 2 * rows] * (0.25 / (2.0 * PUP))
        cosine, sine = turns_sincos((us * xs).astype(jnp.float32) * scale)
        return jnp.concatenate(
            [jnp.where(real, cosine, sine), jnp.where(real, -sine, cosine)], axis=0
        ).astype(jnp.bfloat16)

    def open_slab(slab):
        def openings(g, c):
            r = pl.multiple_of(g * GROUP, GROUP)
            x = 2 * (slab * rows + r + lax.broadcasted_iota(jnp.int32, (GROUP, PUP), 0)) - PUP + 1
            y = 2 * lax.broadcasted_iota(jnp.int32, (GROUP, PUP), 1) - PUP + 1
            radius = x * x + y * y
            inner = 61 * PUP // 100
            inside = (radius <= PUP * PUP) & (radius >= inner * inner)
            opening[pl.ds(r, GROUP), :] = inside.astype(jnp.float32).astype(jnp.bfloat16)
            return c

        lax.fori_loop(0, rows // GROUP, openings, 0)
        for field in (efield0, efield1):
            field[...] = jnp.zeros_like(field)

    def slab_paths(slab):
        mix = mix_ref[pl.ds(pl.multiple_of(side * fields * GROUP, GROUP), fields * GROUP), :]

        def paths(i, c):
            pair = [whole[slab, pl.ds((2 * i + b) * count, count)].reshape(count * GROUP, LANES) for b in range(2)]
            diff = jnp.dot(mix, jnp.concatenate(pair, axis=1), preferred_element_type=jnp.float32)
            for b in range(2):
                path[:, 2 * i + b] = diff[:, b * LANES : (b + 1) * LANES].reshape(fields, GROUP, LANES)
            return c

        tile_pairs = 0
        for number, tiles in enumerate(layout):
            tile_pairs = jnp.where(slab == number, (len(tiles) + 1) // 2, tile_pairs)
        lax.fori_loop(0, tile_pairs, paths, 0)

    def fill(field, tiles, f, inv):
        for t, (group, columns) in enumerate(tiles):
            r = group * GROUP
            cosine, sine = turns_sincos(path[f, t] * inv, SHORT_SIN, SHORT_COS)
            cosine, sine = cosine.astype(jnp.bfloat16), sine.astype(jnp.bfloat16)
            for c in columns:
                lanes = slice(c * LANES, (c + 1) * LANES)
                hole = opening[r : r + GROUP, lanes]
                field[r : r + GROUP, lanes] = cosine * hole
                field[rows + r : rows + r + GROUP, lanes] = sine * hole

    def inverse_tile(wave):
        inv = inverse[wave]
        return jnp.concatenate([inv[:, :LANES], inv[:, :LANES]], axis=0)

    def accumulate(kernel, field, wave, f):
        part_sum = jnp.dot(kernel, field[...], preferred_element_type=jnp.float32)
        here = pl.ds(f * upix, upix)
        image[wave, here, :PUP] += part_sum[:upix]
        image[wave, here, PUP:] += part_sum[upix:]

    def handle(event):
        stage, o, c = event
        if stage == 1:
            first_landed(o, c).wait_recv()
            for e in range(1, 3 if relay else chips):
                plane_copy(o, c, e).start()
            if o + 1 < slabs:
                first_copy(o + 1, c).start()
        if stage == 2 and relay:
            plane_landed(o, c, 1).wait_recv()
            plane_copy(o, c, 3).start()
        if stage == 3:
            for e in range(2 if relay else 1, chips):
                plane_landed(o, c, e).wait_recv()
            core_copy(o, c, core).start()
        if stage == 4:
            for each in range(CHUNKS):
                core_copy(o, each, 1 - core).wait_recv()

    efields = (efield0, efield1)
    plan = scheduled_events(slabs, waves)
    last_step = (slabs - 1) * waves

    def step_body(step, carry):
        order = step // waves
        wave = step % waves
        slab = from_slab(order)

        if kept_tables:

            @pl.when(step == waves)
            def _():
                def make(l, c):
                    second_table(l, l)
                    return c

                lax.fori_loop(0, waves, make, 0)

        for at, events in plan.items():
            if at < last_step:

                @pl.when(step == at)
                def _():
                    for event in events:
                        handle(event)

        @pl.when(wave == 0)
        def _():
            slab_paths(slab)
            open_slab(slab)

        kernel = x_table(slab, wave)
        inv = inverse_tile(wave)

        def units(tiles):
            for f in range(fields):
                fill(efields[f % 2], tiles, f, inv)
                if f > 0:
                    accumulate(kernel, efields[(f - 1) % 2], wave, f - 1)
            accumulate(kernel, efields[(fields - 1) % 2], wave, fields - 1)

        for number, tiles in enumerate(layout):
            pl.when(slab == number)(functools.partial(units, tiles))

        return carry

    lax.fori_loop(0, last_step, step_body, 0)

    last = from_slab(slabs - 1)

    def make_x(l, c):
        xtables[l] = x_table(last, l)
        return c

    lax.fori_loop(0, waves, make_x, 0)
    open_slab(last)
    for event in plan[last_step]:
        handle(event)
    slab_paths(last)

    def sum_copy(f, shift):
        at = (f, shift - 1)
        return remote(
            total.at[f], arrived.at[shift - 1, f], sum_send.at[at], sum_recv.at[at], {"wave": (me + 2 * shift) % slabs}
        )

    def out_copy(f):
        return remote(staged.at[f], out_ref.at[side * fields + f], out_send.at[f], out_recv.at[f], partner)

    def out_landed(f):
        ref = out_ref.at[(1 - side) * fields + f]
        return remote(ref, ref, out_send.at[f], out_recv.at[f], partner)

    def last_fields(f):
        def two_waves(i, c):
            def units(tiles):
                for b in range(2):
                    fill(efields[b], tiles, f, inverse_tile(2 * i + b))
                    if b > 0:
                        accumulate(xtables[2 * i], efield0, 2 * i, f)
                accumulate(xtables[2 * i + 1], efield1, 2 * i + 1, f)

            for number, tiles in enumerate(layout):
                pl.when(last == number)(functools.partial(units, tiles))
            return c

        lax.fori_loop(0, waves // 2, two_waves, 0)

        def finish(wave, c):
            if not kept_tables:
                second_table(wave, 0)
            here = pl.ds(pl.multiple_of(f * upix, GROUP), upix)
            field = jnp.dot(
                image[wave, here, :].astype(jnp.bfloat16),
                tables[wave if kept_tables else 0],
                preferred_element_type=jnp.float32,
            )
            re, im = field[:, :PIX], field[:, PIX:]
            bright = re * re + im * im
            power[wave, here, :] = bright
            total[f, pl.ds(wave, 1), :] = jnp.broadcast_to(
                jnp.sum(jnp.sum(bright, axis=0, keepdims=True), axis=1, keepdims=True), (1, PIX)
            )
            return c

        lax.fori_loop(0, waves, finish, 0)
        for d in range(1, pairs):
            sum_copy(f, d).start()

    def mix_field(f):
        everything = total[f]
        for d in range(1, pairs):
            sum_copy(f, d).wait()
            everything = everything + arrived[d - 1, f]
        level_all = 1.0 / (everything * (1.0 / (PIX * PIX)) + EPSILON)
        levels = [level_all[l : l + 1, :] for l in range(waves)]
        step = 16

        def rows_of(first, store):
            def chunk(i, c):
                r = pl.multiple_of(i * step, step)
                sums = [None] * templates
                for l in range(waves):
                    bright = power[l, pl.ds(pl.multiple_of(f * upix + first, step) + r, step), :]
                    spectrum = (bright * levels[l]).astype(jnp.bfloat16).astype(jnp.float32)
                    for j in range(templates):
                        term = spectrum * weight_ref[((side * fields + f) * templates + j) * waves + l]
                        sums[j] = term if l == 0 else sums[j] + term
                for j in range(templates):
                    store(j, r, sums[j].astype(jnp.bfloat16))
                return c

            lax.fori_loop(0, upix // 2 // step, chunk, 0)

        def to_partner(j, r, value):
            staged[f, j, pl.ds(r, step), :] = value

        def to_own(j, r, value):
            out_ref[side * fields + f, j, pl.ds(r, step), :] = value

        rows_of((1 - side) * (upix // 2), to_partner)
        out_copy(f).start()
        rows_of(side * (upix // 2), to_own)

    def tail(f, carry):
        last_fields(f)

        @pl.when(f > 0)
        def _():
            mix_field(f - 1)

        return carry

    lax.fori_loop(0, fields, tail, 0)
    mix_field(fields - 1)
    for f in range(fields):
        out_landed(f).wait_recv()
        out_copy(f).wait_send()

    for d in range(1, slabs):
        length_copy(d, me).wait_send()
    for o in range(1, slabs):
        for c in range(CHUNKS):
            first_copy(o, c).wait_send()
            for e in range(1, chips):
                plane_copy(o, c, e).wait_send()
            core_copy(o, c, core).wait_send()


def local(sizes, waves, mode_basis, coef_table, table_index, wave_lengths, sed_table, template_ids):
    slabs, field_parts, group_parts = sizes
    count, rows, _ = mode_basis.shape
    fields, templates = template_ids.shape
    upix = 2 * PIX // slabs
    half = fields // 2
    chips = field_parts * group_parts // 2
    tiles = max(len(t) for t in packed_tiles(slabs, rows))
    share = -(-tiles * count // (2 * CHUNKS * chips))
    even = tiles + tiles % 2
    units = max(share * 2 * CHUNKS * chips, even * count)

    coeffs = jnp.take(coef_table, table_index, axis=0, mode="clip")
    same = jnp.eye(GROUP, dtype=jnp.bfloat16)
    mix = (coeffs[:, None, :, None] * same[None, :, None, :]).reshape(fields * GROUP, -1)
    raw = jnp.take(sed_table, template_ids, axis=0, mode="clip")
    weights = (raw / jnp.sum(raw, axis=2, keepdims=True)).astype(jnp.bfloat16).astype(jnp.float32)
    hops = slabs - 1
    others = slabs // 2 - 1
    dma = pltpu.SemaphoreType.DMA

    return pl.pallas_call(
        functools.partial(psf_kernel, sizes, waves, half, share),
        in_specs=[
            pl.BlockSpec(memory_space=pltpu.VMEM),
            pl.BlockSpec(memory_space=pltpu.SMEM),
            pl.BlockSpec(memory_space=pltpu.SMEM),
            pl.BlockSpec(memory_space=pl.ANY),
        ],
        out_specs=pl.BlockSpec(memory_space=pltpu.VMEM),
        out_shape=jax.ShapeDtypeStruct((fields, templates, upix // 2, PIX), jnp.bfloat16),
        scratch_shapes=[
            pltpu.VMEM((count, rows, PUP), jnp.bfloat16),
            pltpu.VMEM((slabs, units, GROUP, LANES), jnp.bfloat16),
            pltpu.VMEM((waves, 8, max(2 * rows, PIX)), jnp.float32),
            pltpu.VMEM((half, even, GROUP, LANES), jnp.float32),
            pltpu.VMEM((waves, half * upix, 2 * PUP), jnp.float32),
            pltpu.VMEM((waves if waves <= 8 else 1, 2 * PUP, 2 * PIX), jnp.bfloat16),
            pltpu.VMEM((waves, 2 * upix, 2 * rows), jnp.bfloat16),
            pltpu.VMEM((2 * rows, PUP), jnp.bfloat16),
            pltpu.VMEM((2 * rows, PUP), jnp.bfloat16),
            pltpu.VMEM((rows, PUP), jnp.bfloat16),
            pltpu.VMEM((waves, half * upix, PIX), jnp.float32),
            pltpu.VMEM((half, waves, PIX), jnp.float32),
            pltpu.VMEM((others, half, waves, PIX), jnp.float32),
            pltpu.VMEM((half, templates, upix // 2, PIX), jnp.bfloat16),
            dma,
            dma((hops,)),
            dma((hops,)),
            dma((hops, CHUNKS)),
            dma((hops, CHUNKS)),
            dma((hops, CHUNKS, chips - 1)),
            dma((hops, CHUNKS, chips - 1)),
            dma((hops, CHUNKS)),
            dma((hops, CHUNKS)),
            dma((half, others)),
            dma((half, others)),
            dma((half,)),
            dma((half,)),
        ],
        compiler_params=pltpu.CompilerParams(
            vmem_limit_bytes=60 * 2**20, collective_id=0, has_side_effects=True
        ),
    )(mix, weights.reshape(-1), wave_lengths, mode_basis)


def solution(mesh):
    sizes = (mesh.shape["wave"], mesh.shape["field"], mesh.shape["groups"])


    def whole_program(*args):
        return sharded(mesh, functools.partial(local, sizes, args[3].shape[0]))(*args)

    return whole_program


def sharded(mesh, body):
    return jax.shard_map(
        body,
        mesh=mesh,
        in_specs=(
            P(None, "wave", None),
            P(),
            P(("groups", "field")),
            P("wave"),
            P(),
            P(("groups", "field"), None),
        ),
        out_specs=P(("groups", "field"), None, "wave", None),
        check_vma=False,
    )
```

```python
import functools

import jax
import jax.numpy as jnp
import numpy as np
from jax import lax
from jax.experimental import pallas as pl
from jax.experimental.pallas import tpu as pltpu
from jax.sharding import PartitionSpec as P

PUP = 512
PIX = 256
EPSILON = 1e-06
GROUP = 16
LANES = 128
WIDE = 256
CHUNKS = 2
AHEAD = 4
BATCH = 6
ROUNDER = 12582912.0

SIN = (4.442879676818848, -7.307816505432129, 3.5977742671966553, -0.7911993861198425)
COS = (1.4142135381698608, -6.978850841522217, 5.739460468292236, -1.883557915687561, 0.3106880187988281)
SHORT_SIN = (4.440917015075684, -7.256804466247559, 3.229630470275879)
SHORT_COS = (1.414183259010315, -6.976953506469727, 5.709674835205078, -1.7155721187591553)


def horner(coefficients, s):
    value = coefficients[-1]
    for c in coefficients[-2::-1]:
        value = c + s * value
    return value


def turns_sincos(turns, sine=SIN, cosine=COS):
    nearest = (turns + ROUNDER) - ROUNDER
    r = turns - nearest
    s = r * r
    a = r * horner(sine, s)
    b = horner(cosine, s)
    return 1.0 - a * a, a * b


def packed_tiles(slabs, rows):
    pos = 2 * np.arange(PUP) - PUP + 1
    radius = pos[:, None] ** 2 + pos[None, :] ** 2
    inside = (radius <= PUP * PUP) & (radius >= (61 * PUP // 100) ** 2)
    columns = PUP // LANES
    half = LANES // 2
    result = []
    for slab in range(slabs):
        tiles = []
        for group in range(rows // GROUP):
            first = slab * rows + group * GROUP
            need = inside[first : first + GROUP].any(axis=0).reshape(columns, LANES)
            low, high = need[:, :half].any(axis=1), need[:, half:].any(axis=1)
            lows = [c for c in range(columns) if low[c] and not high[c]]
            highs = [c for c in range(columns) if high[c] and not low[c]]
            pairs = list(zip(lows, highs))
            for c in range(columns):
                if low[c] and high[c]:
                    tiles.append((group, (c,)))
            tiles += [(group, pair) for pair in pairs]
            tiles += [(group, (c,)) for c in lows[len(pairs) :] + highs[len(pairs) :]]
        result.append(tuple(tiles))
    return result


def hop(order, slabs):
    odd = order % 2
    return odd * ((order + 1) // 2) + (1 - odd) * (slabs - order // 2)


def scheduled_events(slabs, waves):
    timed = []

    def add(block, eighth, *event):
        timed.append(((block * waves + eighth * waves // 8, eighth != 8, len(timed)), event))

    for o in range(1, slabs):
        if o == 1:
            for eighth, event in ((2, (1, 1, 0)), (4, (1, 1, 1)), (5, (2, 1, 0)), (7, (2, 1, 1))):
                add(0, eighth, *event)
            add(0, 8, 3, 1, 0)
            add(0, 8, 3, 1, 1)
            add(0, 8, 4, 1, 0)
        elif o == 2:
            add(0, 7, 1, 2, 0)
            add(0, 7, 1, 2, 1)
            add(1, 0, 2, 2, 0)
            add(1, 2, 2, 2, 1)
            add(1, 2, 3, 2, 0)
            add(1, 6, 3, 2, 1)
            add(1, 8, 4, 2, 0)
        else:
            add(o - 2, 0, 1, o, 0)
            add(o - 2, 5, 1, o, 1)
            add(o - 2, 6, 2, o, 0)
            add(o - 1, 0, 2, o, 1)
            add(o - 1, 4, 3, o, 0)
            add(o - 1, 4, 3, o, 1)
            add(o - 1, 8, 4, o, 0)
    plan = {}
    for (step, *_), event in sorted(timed):
        plan.setdefault(step, []).append(event)
    return plan


def one_hot(targets, rows, columns):
    row = lax.broadcasted_iota(jnp.int32, (rows, columns), 0)
    wanted = jnp.zeros((rows, columns), jnp.int32)
    for i, target in enumerate(targets):
        wanted = jnp.where(row == i, target, wanted)
    column = lax.broadcasted_iota(jnp.int32, (rows, columns), 1)
    return (column == wanted).astype(jnp.float32).astype(jnp.bfloat16)


def same_place(shape, row_shift, column_shift, row_mask=-1, column_mask=-1):
    row = (lax.broadcasted_iota(jnp.int32, shape, 0) >> row_shift) & row_mask
    column = (lax.broadcasted_iota(jnp.int32, shape, 1) >> column_shift) & column_mask
    return (row == column).astype(jnp.float32)


def last_with_last(a, b):
    return lax.dot_general(a, b, (((1,), (1,)), ((), ())), preferred_element_type=jnp.float32)


def gather_parameters(side, fields, templates, waves, count, coef_ref, sed_ref, index_ref, ids_ref, mix, weights):
    bf16 = jnp.bfloat16
    wanted = one_hot([index_ref[side * fields + f] for f in range(fields)], 8 * -(-fields // 8), coef_ref.shape[1])
    coeffs = last_with_last(wanted, coef_ref[...])[:fields].astype(bf16)
    bits = GROUP.bit_length() - 1
    tall = same_place((fields * GROUP, fields), bits, 0).astype(bf16)
    wide = same_place((count, count * GROUP), 0, bits).astype(bf16)
    spread = jnp.dot(tall, coeffs, preferred_element_type=jnp.float32).astype(bf16)
    spread = jnp.dot(spread, wide, preferred_element_type=jnp.float32)
    mix[...] = (spread * same_place(spread.shape, 0, 0, GROUP - 1, GROUP - 1)).astype(bf16)

    ids = [ids_ref[side * fields + f, j] for f in range(fields) for j in range(templates)]
    wanted = one_hot(ids, fields * templates, sed_ref.shape[1])
    table = sed_ref[...]
    high = table.astype(bf16)
    middle = (table - high.astype(jnp.float32)).astype(bf16)
    low = (table - high.astype(jnp.float32) - middle.astype(jnp.float32)).astype(bf16)
    raw = last_with_last(wanted, high) + last_with_last(wanted, middle) + last_with_last(wanted, low)
    shares = (raw / jnp.sum(raw, axis=1, keepdims=True)).astype(bf16)
    bits = PIX.bit_length() - 1
    weights[...] = jnp.dot(shares, same_place((waves, waves * PIX), 0, bits).astype(bf16), preferred_element_type=jnp.float32)


def psf_kernel(
    sizes, waves, fields, share, coef_ref, sed_ref, index_ref, ids_ref, length_ref, basis_ref, out_ref,
    mix, weights, held, whole, inverse, path, image, tables, xtables, efield0, efield1, opening, power, total, arrived, staged,
    local_sem, wl_send, wl_recv, send1, recv1, send2, recv2, send3, recv3, sum_send, sum_recv, out_send, out_recv,
):
    slabs, field_parts, group_parts = sizes
    count, rows, _ = basis_ref.shape
    upix = 2 * PIX // slabs
    own_waves = waves // slabs
    pairs = slabs // 2
    x_parts = field_parts // 2
    chips = x_parts * group_parts
    templates = out_ref.shape[1]
    layout = packed_tiles(slabs, rows)
    kept_tables = tables.shape[0] == waves

    me = lax.axis_index("wave")
    part = lax.axis_index("field")
    core = part % 2
    chip = lax.axis_index("groups") * x_parts + part // 2
    side = me % 2
    first_pix = (me // 2) * upix
    partner = {"wave": me + 1 - 2 * side}

    def wave_peer(shift):
        return {"wave": (me + shift) % slabs}

    def chip_device(other):
        return {"groups": other // x_parts, "field": (other % x_parts) * 2 + core}

    sibling = {"field": part + 1 - 2 * core}

    def remote(src, dst, send, recv, device):
        return pltpu.make_async_remote_copy(
            src_ref=src, dst_ref=dst, send_sem=send, recv_sem=recv,
            device_id=device, device_id_type=pl.DeviceIdType.MESH,
        )

    def from_slab(order):
        return (me + 2 * slabs - hop(order, slabs)) % slabs

    def block(slab, of_core, chunk, of_chip, pieces=1):
        first = ((of_core * CHUNKS + chunk) * chips + of_chip) * share
        return whole.at[slab, pl.ds(first, pieces * share)]

    def first_copy(order, chunk):
        ref = block(me, core, chunk, chip)
        at = (order - 1, chunk)
        return remote(ref, ref, send1.at[at], recv1.at[at], wave_peer(hop(order, slabs)))

    def first_landed(order, chunk):
        ref = block(from_slab(order), core, chunk, chip)
        at = (order - 1, chunk)
        return remote(ref, ref, send1.at[at], recv1.at[at], wave_peer(hop(order, slabs)))

    relay = x_parts == 2 and group_parts == 2
    chip_x, chip_y = chip % x_parts, chip // x_parts
    flip_x, flip_y = 1 - 2 * chip_x, 1 - 2 * chip_y
    first_chip = (chip_y + core * flip_y) * x_parts + chip_x + (1 - core) * flip_x
    second_chip = (chip_y + (1 - core) * flip_y) * x_parts + chip_x + core * flip_x

    def plane_copy(order, chunk, shift):
        at = (order - 1, chunk, shift - 1)
        slab = from_slab(order)
        if relay:
            ref = block(slab, core, chunk, first_chip if shift == 3 else chip)
            device = chip_device(first_chip if shift == 1 else second_chip)
        else:
            ref = block(slab, core, chunk, chip)
            device = chip_device((chip + shift) % chips)
        return remote(ref, ref, send2.at[at], recv2.at[at], device)

    def plane_landed(order, chunk, shift):
        at = (order - 1, chunk, shift - 1)
        if relay:
            sender = (first_chip, second_chip, chips - 1 - chip)[shift - 1]
        else:
            sender = (chip + chips - shift) % chips
        ref = block(from_slab(order), core, chunk, sender)
        return remote(ref, ref, send2.at[at], recv2.at[at], chip_device((chip + shift) % chips))

    def core_copy(order, chunk, which):
        ref = block(from_slab(order), which, chunk, 0, chips)
        at = (order - 1, chunk)
        return remote(ref, ref, send3.at[at], recv3.at[at], sibling)

    def length_copy(shift, sender):
        ref = inverse.at[pl.ds(sender * own_waves, own_waves)]
        return remote(ref, ref, wl_send.at[shift - 1], wl_recv.at[shift - 1], wave_peer(shift))

    barrier = pltpu.get_barrier_semaphore()
    peers = [wave_peer(d) for d in range(1, slabs)] + [chip_device((chip + e) % chips) for e in range(1, chips)] + [sibling]
    for peer in peers:
        pl.semaphore_signal(barrier, inc=1, device_id=peer, device_id_type=pl.DeviceIdType.MESH)
    bring = pltpu.make_async_copy(basis_ref, held, local_sem)
    bring.start()
    for i in range(own_waves):
        inverse[me * own_waves + i] = 1.0 / jnp.full(inverse.shape[1:], length_ref[i], jnp.float32)

    gather_parameters(side, fields, templates, waves, count, coef_ref, sed_ref, index_ref, ids_ref, mix, weights)

    def clear(f, carry):
        for l in range(waves):
            image[l, pl.ds(f * upix, upix), :] = jnp.zeros((upix, 2 * PUP), jnp.float32)
        return carry

    lax.fori_loop(0, fields, clear, 0)
    bring.wait()

    low_lanes = (lax.broadcasted_iota(jnp.int32, (GROUP, LANES), 1) < LANES // 2).astype(jnp.float32)
    low_lanes, high_lanes = low_lanes.astype(jnp.bfloat16), (1.0 - low_lanes).astype(jnp.bfloat16)

    def pack(tiles, k, carry):
        for t, (group, columns) in enumerate(tiles):
            r = group * GROUP
            parts = [held[k, r : r + GROUP, c * LANES : (c + 1) * LANES] for c in columns]
            value = parts[0]
            if len(parts) == 2:
                value = parts[0] * low_lanes + parts[1] * high_lanes
            whole[me, t * count + k] = value
        return carry

    for slab, tiles in enumerate(layout):

        @pl.when(me == slab)
        def _():
            lax.fori_loop(0, count, functools.partial(pack, tiles), 0)

    pl.semaphore_wait(barrier, len(peers))
    for c in range(CHUNKS):
        first_copy(1, c).start()
    for d in range(1, slabs):
        length_copy(d, me).start()
    for d in range(1, slabs):
        length_copy(d, (me + slabs - d) % slabs).wait_recv()

    def second_table(wave, slot):
        scale = inverse[wave][:1, :PIX] * (0.25 / (2.0 * PUP))
        step = 64
        for r in range(0, PUP, step):
            ys = 2 * (r + lax.broadcasted_iota(jnp.int32, (step, PIX), 0)) - PUP + 1
            vs = lax.broadcasted_iota(jnp.int32, (step, PIX), 1) - PIX // 2
            cosine, sine = turns_sincos((ys * vs).astype(jnp.float32) * scale)
            cosine = cosine.astype(jnp.bfloat16)
            tables[slot, r : r + step, :PIX] = cosine
            tables[slot, r : r + step, PIX:] = (-sine).astype(jnp.bfloat16)
            tables[slot, PUP + r : PUP + r + step, :PIX] = sine.astype(jnp.bfloat16)
            tables[slot, PUP + r : PUP + r + step, PIX:] = cosine

    def x_table(slab, wave):
        lane = lax.broadcasted_iota(jnp.int32, (upix, 2 * rows), 1)
        real = lane < rows
        xs = 2 * (slab * rows + jnp.where(real, lane, lane - rows)) - PUP + 1
        us = first_pix + lax.broadcasted_iota(jnp.int32, (upix, 2 * rows), 0) - PIX // 2
        scale = inverse[wave][:1, : 2 * rows] * (0.25 / (2.0 * PUP))
        cosine, sine = turns_sincos((us * xs).astype(jnp.float32) * scale)
        return jnp.concatenate(
            [jnp.where(real, cosine, sine), jnp.where(real, -sine, cosine)], axis=0
        ).astype(jnp.bfloat16)

    def open_slab(slab):
        def openings(g, c):
            r = pl.multiple_of(g * GROUP, GROUP)
            x = 2 * (slab * rows + r + lax.broadcasted_iota(jnp.int32, (GROUP, PUP), 0)) - PUP + 1
            y = 2 * lax.broadcasted_iota(jnp.int32, (GROUP, PUP), 1) - PUP + 1
            radius = x * x + y * y
            inner = 61 * PUP // 100
            inside = (radius <= PUP * PUP) & (radius >= inner * inner)
            opening[pl.ds(r, GROUP), :] = inside.astype(jnp.float32).astype(jnp.bfloat16)
            return c

        lax.fori_loop(0, rows // GROUP, openings, 0)
        for field in (efield0, efield1):
            field[...] = jnp.zeros_like(field)

    def slab_paths(slab):
        def paths(i, c):
            for q in range(BATCH // 2):
                first = BATCH * i + 2 * q
                pair = [whole[slab, pl.ds((first + b) * count, count)].reshape(count * GROUP, LANES) for b in range(2)]
                diff = jnp.dot(mix[...], jnp.concatenate(pair, axis=1), preferred_element_type=jnp.float32)
                for b in range(2):
                    path[:, first + b] = diff[:, b * LANES : (b + 1) * LANES].reshape(fields, GROUP, LANES)
            return c

        batches = 0
        for number, tiles in enumerate(layout):
            batches = jnp.where(slab == number, -(-len(tiles) // BATCH), batches)
        lax.fori_loop(0, batches, paths, 0)

    def fill(field, tiles, f, inv, between=()):
        for t, (group, columns) in enumerate(tiles):
            for i, work in enumerate(between):
                if t == (2 * i + 1) * len(tiles) // (2 * len(between)):
                    work()
            r = group * GROUP
            cosine, sine = turns_sincos(path[f, t] * inv, SHORT_SIN, SHORT_COS)
            cosine, sine = cosine.astype(jnp.bfloat16), sine.astype(jnp.bfloat16)
            for c in columns:
                lanes = slice(c * LANES, (c + 1) * LANES)
                hole = opening[r : r + GROUP, lanes]
                field[r : r + GROUP, lanes] = cosine * hole
                field[rows + r : rows + r + GROUP, lanes] = sine * hole

    def inverse_tile(wave):
        inv = inverse[wave]
        return jnp.concatenate([inv[:, :LANES], inv[:, :LANES]], axis=0)

    def accumulation(kernel, field, wave, f):
        here = pl.ds(f * upix, upix)

        def part(n):
            lanes = slice(n, n + WIDE)
            part_sum = jnp.dot(kernel, field[:, lanes], preferred_element_type=jnp.float32)
            image[wave, here, n : n + WIDE] += part_sum[:upix]
            image[wave, here, PUP + n : PUP + n + WIDE] += part_sum[upix:]

        return [functools.partial(part, n) for n in range(0, PUP, WIDE)]

    def handle(event):
        stage, o, c = event
        if stage == 1:
            first_landed(o, c).wait_recv()
            for e in range(1, 3 if relay else chips):
                plane_copy(o, c, e).start()
            if o + 1 < slabs:
                first_copy(o + 1, c).start()
        if stage == 2 and relay:
            plane_landed(o, c, 1).wait_recv()
            plane_copy(o, c, 3).start()
        if stage == 3:
            for e in range(2 if relay else 1, chips):
                plane_landed(o, c, e).wait_recv()
            core_copy(o, c, core).start()
        if stage == 4:
            for each in range(CHUNKS):
                core_copy(o, each, 1 - core).wait_recv()

    efields = (efield0, efield1)
    plan = scheduled_events(slabs, waves)
    last_step = (slabs - 1) * waves

    def step_body(step, carry):
        order = step // waves
        wave = step % waves
        slab = from_slab(order)

        if kept_tables:

            @pl.when(step == waves)
            def _():
                def make(l, c):
                    second_table(l, l)
                    return c

                lax.fori_loop(0, waves, make, 0)

        for at, events in plan.items():
            if at < last_step:

                @pl.when(step == at)
                def _():
                    for event in events:
                        handle(event)

        @pl.when(wave == 0)
        def _():
            slab_paths(slab)
            open_slab(slab)

        kernel = x_table(slab, wave)
        inv = inverse_tile(wave)

        def units(tiles):
            work = []
            for f in range(fields):
                fill(efields[f % 2], tiles, f, inv, work)
                work = accumulation(kernel, efields[f % 2], wave, f)
            for rest in work:
                rest()

        for number, tiles in enumerate(layout):
            pl.when(slab == number)(functools.partial(units, tiles))

        return carry

    lax.fori_loop(0, last_step, step_body, 0)

    last = from_slab(slabs - 1)

    def make_x(l, c):
        xtables[l] = x_table(last, l)
        return c

    lax.fori_loop(0, waves, make_x, 0)
    open_slab(last)
    for event in plan[last_step]:
        handle(event)
    slab_paths(last)

    def sum_copy(f, shift):
        at = (f, shift - 1)
        return remote(
            total.at[f], arrived.at[shift - 1, f], sum_send.at[at], sum_recv.at[at], {"wave": (me + 2 * shift) % slabs}
        )

    def out_copy(f):
        return remote(staged.at[f], out_ref.at[side * fields + f], out_send.at[f], out_recv.at[f], partner)

    def out_landed(f):
        ref = out_ref.at[(1 - side) * fields + f]
        return remote(ref, ref, out_send.at[f], out_recv.at[f], partner)

    def last_units(f):
        def some_waves(i, c):
            def units(tiles):
                work = []
                for b in range(AHEAD):
                    wave = AHEAD * i + b
                    fill(efields[b % 2], tiles, f, inverse_tile(wave), work)
                    work = accumulation(xtables[wave], efields[b % 2], wave, f)
                for rest in work:
                    rest()

            for number, tiles in enumerate(layout):
                pl.when(last == number)(functools.partial(units, tiles))
            return c

        lax.fori_loop(0, waves // AHEAD, some_waves, 0)

    def last_images(f):
        here = pl.ds(pl.multiple_of(f * upix, GROUP), upix)

        def finish(i, c):
            for b in range(AHEAD):
                wave = AHEAD * i + b
                if not kept_tables:
                    second_table(wave, 0)
                field = jnp.dot(
                    image[wave, here, :].astype(jnp.bfloat16),
                    tables[wave if kept_tables else 0],
                    preferred_element_type=jnp.float32,
                )
                re, im = field[:, :PIX], field[:, PIX:]
                bright = re * re + im * im
                power[wave, here, :] = bright
                total[f, pl.ds(wave, 1), :] = jnp.sum(bright, axis=0, keepdims=True)
            return c

        lax.fori_loop(0, waves // AHEAD, finish, 0)
        total[f] = jnp.broadcast_to(jnp.sum(total[f], axis=1, keepdims=True), (waves, PIX))
        for d in range(1, pairs):
            sum_copy(f, d).start()

    def mix_field(f):
        everything = total[f]
        for d in range(1, pairs):
            sum_copy(f, d).wait()
            everything = everything + arrived[d - 1, f]
        level_all = 1.0 / (everything * (1.0 / (PIX * PIX)) + EPSILON)
        levels = [level_all[l : l + 1, :] for l in range(waves)]
        step = 16

        def rows_of(first, store):
            def chunk(i, c):
                r = pl.multiple_of(i * step, step)
                sums = [None] * templates
                for l in range(waves):
                    bright = power[l, pl.ds(pl.multiple_of(f * upix + first, step) + r, step), :]
                    spectrum = (bright * levels[l]).astype(jnp.bfloat16).astype(jnp.float32)
                    for j in range(templates):
                        term = spectrum * weights[pl.ds(f * templates + j, 1), l * PIX : (l + 1) * PIX]
                        sums[j] = term if l == 0 else sums[j] + term
                for j in range(templates):
                    store(j, r, sums[j].astype(jnp.bfloat16))
                return c

            lax.fori_loop(0, upix // 2 // step, chunk, 0)

        def to_partner(j, r, value):
            staged[f, j, pl.ds(r, step), :] = value

        def to_own(j, r, value):
            out_ref[side * fields + f, j, pl.ds(r, step), :] = value

        rows_of((1 - side) * (upix // 2), to_partner)
        out_copy(f).start()
        rows_of(side * (upix // 2), to_own)

    def tail(f, carry):
        last_units(f)

        @pl.when(f > 0)
        def _():
            mix_field(f - 1)

        last_images(f)
        return carry

    lax.fori_loop(0, fields, tail, 0)
    mix_field(fields - 1)
    for f in range(fields):
        out_landed(f).wait_recv()
        out_copy(f).wait_send()

    for d in range(1, slabs):
        length_copy(d, me).wait_send()
    for o in range(1, slabs):
        for c in range(CHUNKS):
            first_copy(o, c).wait_send()
            for e in range(1, chips):
                plane_copy(o, c, e).wait_send()
            core_copy(o, c, core).wait_send()


def local(sizes, waves, mode_basis, coef_table, table_index, wave_lengths, sed_table, template_ids):
    slabs, field_parts, group_parts = sizes
    count, rows, _ = mode_basis.shape
    fields, templates = template_ids.shape
    upix = 2 * PIX // slabs
    half = fields // 2
    chips = field_parts * group_parts // 2
    tiles = max(len(t) for t in packed_tiles(slabs, rows))
    share = -(-tiles * count // (2 * CHUNKS * chips))
    even = -(-tiles // BATCH) * BATCH
    units = max(share * 2 * CHUNKS * chips, even * count)

    hops = slabs - 1
    others = slabs // 2 - 1
    dma = pltpu.SemaphoreType.DMA

    return pl.pallas_call(
        functools.partial(psf_kernel, sizes, waves, half, share),
        in_specs=[
            pl.BlockSpec(memory_space=pltpu.VMEM),
            pl.BlockSpec(memory_space=pltpu.VMEM),
            pl.BlockSpec(memory_space=pltpu.SMEM),
            pl.BlockSpec(memory_space=pltpu.SMEM),
            pl.BlockSpec(memory_space=pltpu.SMEM),
            pl.BlockSpec(memory_space=pl.ANY),
        ],
        out_specs=pl.BlockSpec(memory_space=pltpu.VMEM),
        out_shape=jax.ShapeDtypeStruct((fields, templates, upix // 2, PIX), jnp.bfloat16),
        scratch_shapes=[
            pltpu.VMEM((half * GROUP, count * GROUP), jnp.bfloat16),
            pltpu.VMEM((half * templates, waves * PIX), jnp.float32),
            pltpu.VMEM((count, rows, PUP), jnp.bfloat16),
            pltpu.VMEM((slabs, units, GROUP, LANES), jnp.bfloat16),
            pltpu.VMEM((waves, 8, max(2 * rows, PIX)), jnp.float32),
            pltpu.VMEM((half, even, GROUP, LANES), jnp.float32),
            pltpu.VMEM((waves, half * upix, 2 * PUP), jnp.float32),
            pltpu.VMEM((waves if waves <= 8 else 1, 2 * PUP, 2 * PIX), jnp.bfloat16),
            pltpu.VMEM((waves, 2 * upix, 2 * rows), jnp.bfloat16),
            pltpu.VMEM((2 * rows, PUP), jnp.bfloat16),
            pltpu.VMEM((2 * rows, PUP), jnp.bfloat16),
            pltpu.VMEM((rows, PUP), jnp.bfloat16),
            pltpu.VMEM((waves, half * upix, PIX), jnp.float32),
            pltpu.VMEM((half, waves, PIX), jnp.float32),
            pltpu.VMEM((others, half, waves, PIX), jnp.float32),
            pltpu.VMEM((half, templates, upix // 2, PIX), jnp.bfloat16),
            dma,
            dma((hops,)),
            dma((hops,)),
            dma((hops, CHUNKS)),
            dma((hops, CHUNKS)),
            dma((hops, CHUNKS, chips - 1)),
            dma((hops, CHUNKS, chips - 1)),
            dma((hops, CHUNKS)),
            dma((hops, CHUNKS)),
            dma((half, others)),
            dma((half, others)),
            dma((half,)),
            dma((half,)),
        ],
        compiler_params=pltpu.CompilerParams(
            vmem_limit_bytes=60 * 2**20, collective_id=0, has_side_effects=True
        ),
    )(coef_table.T, sed_table.T, table_index, template_ids, wave_lengths, mode_basis)


def solution(mesh):
    sizes = (mesh.shape["wave"], mesh.shape["field"], mesh.shape["groups"])


    def whole_program(*args):
        return sharded(mesh, functools.partial(local, sizes, args[3].shape[0]))(*args)

    return whole_program


def sharded(mesh, body):
    return jax.shard_map(
        body,
        mesh=mesh,
        in_specs=(
            P(None, "wave", None),
            P(),
            P(("groups", "field")),
            P("wave"),
            P(),
            P(("groups", "field"), None),
        ),
        out_specs=P(("groups", "field"), None, "wave", None),
        check_vma=False,
    )
```

```python
import functools

import jax
import jax.numpy as jnp
import numpy as np
from jax import lax
from jax.experimental import pallas as pl
from jax.experimental.pallas import tpu as pltpu
from jax.sharding import PartitionSpec as P

PUP = 512
PIX = 256
EPSILON = 1e-06
GROUP = 16
LANES = 128
CHUNKS = 2
AHEAD = 4
BATCH = 6
ROUNDER = 12582912.0

SIN = (4.442879676818848, -7.307816505432129, 3.5977742671966553, -0.7911993861198425)
COS = (1.4142135381698608, -6.978850841522217, 5.739460468292236, -1.883557915687561, 0.3106880187988281)
SHORT_SIN = (4.440917015075684, -7.256804466247559, 3.229630470275879)
SHORT_COS = (1.414183259010315, -6.976953506469727, 5.709674835205078, -1.7155721187591553)


def horner(coefficients, s):
    value = coefficients[-1]
    for c in coefficients[-2::-1]:
        value = c + s * value
    return value


def turns_sincos(turns, sine=SIN, cosine=COS):
    nearest = (turns + ROUNDER) - ROUNDER
    r = turns - nearest
    s = r * r
    a = r * horner(sine, s)
    b = horner(cosine, s)
    return 1.0 - a * a, a * b


def packed_tiles(slabs, rows):
    pos = 2 * np.arange(PUP) - PUP + 1
    radius = pos[:, None] ** 2 + pos[None, :] ** 2
    inside = (radius <= PUP * PUP) & (radius >= (61 * PUP // 100) ** 2)
    columns = PUP // LANES
    half = LANES // 2
    result = []
    for slab in range(slabs):
        tiles = []
        for group in range(rows // GROUP):
            first = slab * rows + group * GROUP
            need = inside[first : first + GROUP].any(axis=0).reshape(columns, LANES)
            low, high = need[:, :half].any(axis=1), need[:, half:].any(axis=1)
            lows = [c for c in range(columns) if low[c] and not high[c]]
            highs = [c for c in range(columns) if high[c] and not low[c]]
            pairs = list(zip(lows, highs))
            for c in range(columns):
                if low[c] and high[c]:
                    tiles.append((group, (c,)))
            tiles += [(group, pair) for pair in pairs]
            tiles += [(group, (c,)) for c in lows[len(pairs) :] + highs[len(pairs) :]]
        result.append(tuple(tiles))
    return result


def hop(order, slabs):
    odd = order % 2
    return odd * ((order + 1) // 2) + (1 - odd) * (slabs - order // 2)


def scheduled_events(slabs, waves):
    timed = []

    def add(block, eighth, *event):
        timed.append(((block * waves + eighth * waves // 8, eighth != 8, len(timed)), event))

    for o in range(1, slabs):
        if o == 1:
            for eighth, event in ((0, (1, 1, 0)), (1, (1, 1, 1)), (4, (2, 1, 0)), (6, (2, 1, 1)), (7, (3, 1, 0))):
                add(0, eighth, *event)
            if slabs > 2:
                add(0, 7, 1, 2, 0)
            add(0, 8, 3, 1, 1)
            if slabs > 2:
                add(0, 8, 1, 2, 1)
            add(0, 8, 0, 1, 0)
            add(0, 8, 4, 1, 0)
        elif o == 2:
            add(1, 0, 2, 2, 0)
            add(1, 2, 2, 2, 1)
            add(1, 2, 3, 2, 0)
            add(1, 6, 3, 2, 1)
            add(1, 8, 4, 2, 0)
        else:
            add(o - 2, 0, 1, o, 0)
            add(o - 2, 5, 1, o, 1)
            add(o - 2, 6, 2, o, 0)
            add(o - 1, 0, 2, o, 1)
            add(o - 1, 4, 3, o, 0)
            add(o - 1, 4, 3, o, 1)
            add(o - 1, 8, 4, o, 0)
    plan = {}
    for (step, *_), event in sorted(timed):
        plan.setdefault(step, []).append(event)
    return plan


def one_hot(targets, rows, columns):
    row = lax.broadcasted_iota(jnp.int32, (rows, columns), 0)
    wanted = jnp.zeros((rows, columns), jnp.int32)
    for i, target in enumerate(targets):
        wanted = jnp.where(row == i, target, wanted)
    column = lax.broadcasted_iota(jnp.int32, (rows, columns), 1)
    return (column == wanted).astype(jnp.float32).astype(jnp.bfloat16)


def same_place(shape, row_shift, column_shift, row_mask=-1, column_mask=-1):
    row = (lax.broadcasted_iota(jnp.int32, shape, 0) >> row_shift) & row_mask
    column = (lax.broadcasted_iota(jnp.int32, shape, 1) >> column_shift) & column_mask
    return (row == column).astype(jnp.float32)


def last_with_last(a, b):
    return lax.dot_general(a, b, (((1,), (1,)), ((), ())), preferred_element_type=jnp.float32)


def gather_parameters(side, fields, templates, waves, count, coef_ref, sed_ref, index_ref, ids_ref, mix, weights):
    bf16 = jnp.bfloat16
    wanted = one_hot([index_ref[side * fields + f] for f in range(fields)], 8 * -(-fields // 8), coef_ref.shape[1])
    coeffs = last_with_last(wanted, coef_ref[...])[:fields].astype(bf16)
    bits = GROUP.bit_length() - 1
    tall = same_place((fields * GROUP, fields), bits, 0).astype(bf16)
    wide = same_place((count, count * GROUP), 0, bits).astype(bf16)
    spread = jnp.dot(tall, coeffs, preferred_element_type=jnp.float32).astype(bf16)
    spread = jnp.dot(spread, wide, preferred_element_type=jnp.float32)
    mix[...] = (spread * same_place(spread.shape, 0, 0, GROUP - 1, GROUP - 1)).astype(bf16)

    ids = [ids_ref[side * fields + f, j] for f in range(fields) for j in range(templates)]
    wanted = one_hot(ids, fields * templates, sed_ref.shape[1])
    table = sed_ref[...]
    high = table.astype(bf16)
    middle = (table - high.astype(jnp.float32)).astype(bf16)
    low = (table - high.astype(jnp.float32) - middle.astype(jnp.float32)).astype(bf16)
    raw = last_with_last(wanted, high) + last_with_last(wanted, middle) + last_with_last(wanted, low)
    shares = (raw / jnp.sum(raw, axis=1, keepdims=True)).astype(bf16)
    bits = PIX.bit_length() - 1
    weights[...] = jnp.dot(shares, same_place((waves, waves * PIX), 0, bits).astype(bf16), preferred_element_type=jnp.float32)


def psf_kernel(
    sizes, waves, fields, share, coef_ref, sed_ref, index_ref, ids_ref, length_ref, basis_ref, out_ref,
    mix, weights, held, whole, inverse, path, image, tables, xtables, efields, opening, power, total, arrived, staged,
    local_sem, wl_send, wl_recv, send1, recv1, send2, recv2, send3, recv3, sum_send, sum_recv, out_send, out_recv,
):
    slabs, field_parts, group_parts = sizes
    count, rows, _ = basis_ref.shape
    upix = 2 * PIX // slabs
    own_waves = waves // slabs
    pairs = slabs // 2
    x_parts = field_parts // 2
    chips = x_parts * group_parts
    templates = out_ref.shape[1]
    layout = packed_tiles(slabs, rows)
    kept_tables = tables.shape[0] == waves

    me = lax.axis_index("wave")
    part = lax.axis_index("field")
    core = part % 2
    chip = lax.axis_index("groups") * x_parts + part // 2
    side = me % 2
    first_pix = (me // 2) * upix
    partner = {"wave": me + 1 - 2 * side}

    def wave_peer(shift):
        return {"wave": (me + shift) % slabs}

    def chip_device(other):
        return {"groups": other // x_parts, "field": (other % x_parts) * 2 + core}

    sibling = {"field": part + 1 - 2 * core}

    def remote(src, dst, send, recv, device):
        return pltpu.make_async_remote_copy(
            src_ref=src, dst_ref=dst, send_sem=send, recv_sem=recv,
            device_id=device, device_id_type=pl.DeviceIdType.MESH,
        )

    def from_slab(order):
        return (me + 2 * slabs - hop(order, slabs)) % slabs

    def block(slab, of_core, chunk, of_chip, pieces=1):
        first = ((of_core * CHUNKS + chunk) * chips + of_chip) * share
        return whole.at[slab, pl.ds(first, pieces * share)]

    def first_copy(order, chunk):
        ref = block(me, core, chunk, chip)
        at = (order - 1, chunk)
        return remote(ref, ref, send1.at[at], recv1.at[at], wave_peer(hop(order, slabs)))

    def first_landed(order, chunk):
        ref = block(from_slab(order), core, chunk, chip)
        at = (order - 1, chunk)
        return remote(ref, ref, send1.at[at], recv1.at[at], wave_peer(hop(order, slabs)))

    relay = x_parts == 2 and group_parts == 2
    chip_x, chip_y = chip % x_parts, chip // x_parts
    flip_x, flip_y = 1 - 2 * chip_x, 1 - 2 * chip_y
    first_chip = (chip_y + core * flip_y) * x_parts + chip_x + (1 - core) * flip_x
    second_chip = (chip_y + (1 - core) * flip_y) * x_parts + chip_x + core * flip_x

    def plane_copy(order, chunk, shift):
        at = (order - 1, chunk, shift - 1)
        slab = from_slab(order)
        if relay:
            ref = block(slab, core, chunk, first_chip if shift == 3 else chip)
            device = chip_device(first_chip if shift == 1 else second_chip)
        else:
            ref = block(slab, core, chunk, chip)
            device = chip_device((chip + shift) % chips)
        return remote(ref, ref, send2.at[at], recv2.at[at], device)

    def plane_landed(order, chunk, shift):
        at = (order - 1, chunk, shift - 1)
        if relay:
            sender = (first_chip, second_chip, chips - 1 - chip)[shift - 1]
        else:
            sender = (chip + chips - shift) % chips
        ref = block(from_slab(order), core, chunk, sender)
        return remote(ref, ref, send2.at[at], recv2.at[at], chip_device((chip + shift) % chips))

    def core_copy(order, chunk, which):
        ref = block(from_slab(order), which, chunk, 0, chips)
        at = (order - 1, chunk)
        return remote(ref, ref, send3.at[at], recv3.at[at], sibling)

    def length_copy(shift, sender):
        ref = inverse.at[pl.ds(sender * own_waves, own_waves)]
        return remote(ref, ref, wl_send.at[shift - 1], wl_recv.at[shift - 1], wave_peer(shift))

    barrier = pltpu.get_barrier_semaphore()
    peers = [wave_peer(d) for d in range(1, slabs)] + [chip_device((chip + e) % chips) for e in range(1, chips)] + [sibling]
    for peer in peers:
        pl.semaphore_signal(barrier, inc=1, device_id=peer, device_id_type=pl.DeviceIdType.MESH)
    bring = pltpu.make_async_copy(basis_ref, held, local_sem)
    bring.start()
    for i in range(own_waves):
        inverse[me * own_waves + i] = 1.0 / jnp.full(inverse.shape[1:], length_ref[i], jnp.float32)

    def clear(f, carry):
        for l in range(waves):
            image[l, pl.ds(f * upix, upix), :] = jnp.zeros((upix, 2 * PUP), jnp.float32)
        return carry

    bring.wait()

    low_lanes = (lax.broadcasted_iota(jnp.int32, (GROUP, LANES), 1) < LANES // 2).astype(jnp.float32)
    low_lanes, high_lanes = low_lanes.astype(jnp.bfloat16), (1.0 - low_lanes).astype(jnp.bfloat16)

    def pack(tiles, k, carry):
        for t, (group, columns) in enumerate(tiles):
            r = group * GROUP
            parts = [held[k, r : r + GROUP, c * LANES : (c + 1) * LANES] for c in columns]
            value = parts[0]
            if len(parts) == 2:
                value = parts[0] * low_lanes + parts[1] * high_lanes
            whole[me, t * count + k] = value
        return carry

    for slab, tiles in enumerate(layout):

        @pl.when(me == slab)
        def _():
            lax.fori_loop(0, count, functools.partial(pack, tiles), 0)

    pl.semaphore_wait(barrier, len(peers))
    for c in range(CHUNKS):
        first_copy(1, c).start()
    for d in range(1, slabs):
        length_copy(d, me).start()
    gather_parameters(side, fields, templates, waves, count, coef_ref, sed_ref, index_ref, ids_ref, mix, weights)
    lax.fori_loop(0, fields, clear, 0)
    for d in range(1, slabs):
        length_copy(d, (me + slabs - d) % slabs).wait_recv()

    def second_table(wave, slot):
        scale = inverse[wave][:1, :PIX] * (0.25 / (2.0 * PUP))
        step = 64
        for r in range(0, PUP, step):
            ys = 2 * (r + lax.broadcasted_iota(jnp.int32, (step, PIX), 0)) - PUP + 1
            vs = lax.broadcasted_iota(jnp.int32, (step, PIX), 1) - PIX // 2
            cosine, sine = turns_sincos((ys * vs).astype(jnp.float32) * scale)
            cosine = cosine.astype(jnp.bfloat16)
            tables[slot, r : r + step, :PIX] = cosine
            tables[slot, r : r + step, PIX:] = (-sine).astype(jnp.bfloat16)
            tables[slot, PUP + r : PUP + r + step, :PIX] = sine.astype(jnp.bfloat16)
            tables[slot, PUP + r : PUP + r + step, PIX:] = cosine

    def x_table(slab, wave):
        xs = 2 * (slab * rows + lax.broadcasted_iota(jnp.int32, (upix, rows), 1)) - PUP + 1
        us = first_pix + lax.broadcasted_iota(jnp.int32, (upix, rows), 0) - PIX // 2
        scale = inverse[wave][:1, :rows] * (0.25 / (2.0 * PUP))
        cosine, sine = turns_sincos((us * xs).astype(jnp.float32) * scale)
        upper = jnp.concatenate([cosine, sine], axis=1)
        lower = jnp.concatenate([-sine, cosine], axis=1)
        return jnp.concatenate([upper, lower], axis=0).astype(jnp.bfloat16)

    def open_slab(slab):
        def openings(g, c):
            r = pl.multiple_of(g * GROUP, GROUP)
            x = 2 * (slab * rows + r + lax.broadcasted_iota(jnp.int32, (GROUP, PUP), 0)) - PUP + 1
            y = 2 * lax.broadcasted_iota(jnp.int32, (GROUP, PUP), 1) - PUP + 1
            radius = x * x + y * y
            inner = 61 * PUP // 100
            inside = (radius <= PUP * PUP) & (radius >= inner * inner)
            opening[pl.ds(r, GROUP), :] = inside.astype(jnp.float32).astype(jnp.bfloat16)
            return c

        lax.fori_loop(0, rows // GROUP, openings, 0)
        for i in range(efields.shape[0]):
            efields[i] = jnp.zeros(efields.shape[1:], efields.dtype)

    def slab_paths(slab):
        def paths(i, c):
            for q in range(BATCH // 2):
                first = BATCH * i + 2 * q
                pair = [whole[slab, pl.ds((first + b) * count, count)].reshape(count * GROUP, LANES) for b in range(2)]
                diff = jnp.dot(mix[...], jnp.concatenate(pair, axis=1), preferred_element_type=jnp.float32)
                for b in range(2):
                    path[:, first + b] = diff[:, b * LANES : (b + 1) * LANES].reshape(fields, GROUP, LANES)
            return c

        batches = 0
        for number, tiles in enumerate(layout):
            batches = jnp.where(slab == number, -(-len(tiles) // BATCH), batches)
        lax.fori_loop(0, batches, paths, 0)

    def fill(field, tiles, f, inv):
        for t, (group, columns) in enumerate(tiles):
            r = group * GROUP
            cosine, sine = turns_sincos(path[f, t] * inv, SHORT_SIN, SHORT_COS)
            cosine, sine = cosine.astype(jnp.bfloat16), sine.astype(jnp.bfloat16)
            for c in columns:
                lanes = slice(c * LANES, (c + 1) * LANES)
                hole = opening[r : r + GROUP, lanes]
                efields[field, r : r + GROUP, lanes] = cosine * hole
                efields[field, rows + r : rows + r + GROUP, lanes] = sine * hole

    def inverse_tile(wave):
        inv = inverse[wave]
        return jnp.concatenate([inv[:, :LANES], inv[:, :LANES]], axis=0)

    def accumulate(kernel, field, wave, f):
        part_sum = jnp.dot(kernel, efields[field], preferred_element_type=jnp.float32)
        here = pl.ds(f * upix, upix)
        image[wave, here, :PUP] += part_sum[:upix]
        image[wave, here, PUP:] += part_sum[upix:]

    def handle(event):
        stage, o, c = event
        if stage == 0 and kept_tables:
            def make(l, carry):
                second_table(l, l)
                return carry

            lax.fori_loop(0, waves, make, 0)
        if stage == 1:
            first_landed(o, c).wait_recv()
            for e in range(1, 3 if relay else chips):
                plane_copy(o, c, e).start()
            if o + 1 < slabs:
                first_copy(o + 1, c).start()
        if stage == 2 and relay:
            plane_landed(o, c, 1).wait_recv()
            plane_copy(o, c, 3).start()
        if stage == 3:
            for e in range(2 if relay else 1, chips):
                plane_landed(o, c, e).wait_recv()
            core_copy(o, c, core).start()
        if stage == 4:
            for each in range(CHUNKS):
                core_copy(o, each, 1 - core).wait_recv()

    plan = scheduled_events(slabs, waves)
    last_step = (slabs - 1) * waves

    def step_body(step, carry):
        order = step // waves
        wave = step % waves
        slab = from_slab(order)

        for at, events in plan.items():
            if at < last_step:

                @pl.when(step == at)
                def _():
                    for event in events:
                        handle(event)

        @pl.when(wave == 0)
        def _():
            slab_paths(slab)
            open_slab(slab)

        kernel = x_table(slab, wave)
        inv = inverse_tile(wave)

        def units(tiles):
            for f in range(fields):
                fill(f, tiles, f, inv)
            for f in range(fields):
                accumulate(kernel, f, wave, f)

        for number, tiles in enumerate(layout):
            pl.when(slab == number)(functools.partial(units, tiles))

        return carry

    lax.fori_loop(0, last_step, step_body, 0)

    last = from_slab(slabs - 1)

    def make_x(l, c):
        xtables[l] = x_table(last, l)
        return c

    lax.fori_loop(0, waves, make_x, 0)
    open_slab(last)
    for event in plan[last_step]:
        handle(event)
    slab_paths(last)

    def sum_copy(f, shift):
        at = (f, shift - 1)
        return remote(
            total.at[f], arrived.at[shift - 1, f], sum_send.at[at], sum_recv.at[at], {"wave": (me + 2 * shift) % slabs}
        )

    def out_copy(f):
        return remote(staged.at[f], out_ref.at[side * fields + f], out_send.at[f], out_recv.at[f], partner)

    def out_landed(f):
        ref = out_ref.at[(1 - side) * fields + f]
        return remote(ref, ref, out_send.at[f], out_recv.at[f], partner)

    def last_units(f):
        def some_waves(i, c):
            def units(tiles):
                for b in range(AHEAD):
                    fill(b, tiles, f, inverse_tile(AHEAD * i + b))
                for b in range(AHEAD):
                    accumulate(xtables[AHEAD * i + b], b, AHEAD * i + b, f)

            for number, tiles in enumerate(layout):
                pl.when(last == number)(functools.partial(units, tiles))
            return c

        lax.fori_loop(0, waves // AHEAD, some_waves, 0)

    def last_images(f):
        here = pl.ds(pl.multiple_of(f * upix, GROUP), upix)

        def finish(i, c):
            for b in range(AHEAD):
                wave = AHEAD * i + b
                if not kept_tables:
                    second_table(wave, 0)
                field = jnp.dot(
                    image[wave, here, :].astype(jnp.bfloat16),
                    tables[wave if kept_tables else 0],
                    preferred_element_type=jnp.float32,
                )
                re, im = field[:, :PIX], field[:, PIX:]
                bright = re * re + im * im
                power[wave, here, :] = bright
                total[f, pl.ds(wave, 1), :] = jnp.sum(bright, axis=0, keepdims=True)
            return c

        lax.fori_loop(0, waves // AHEAD, finish, 0)
        total[f] = jnp.broadcast_to(jnp.sum(total[f], axis=1, keepdims=True), (waves, PIX))
        for d in range(1, pairs):
            sum_copy(f, d).start()

    def mix_field(f):
        everything = total[f]
        for d in range(1, pairs):
            sum_copy(f, d).wait()
            everything = everything + arrived[d - 1, f]
        level_all = 1.0 / (everything * (1.0 / (PIX * PIX)) + EPSILON)
        levels = [level_all[l : l + 1, :] for l in range(waves)]
        step = 16

        def rows_of(first, store):
            def chunk(i, c):
                r = pl.multiple_of(i * step, step)
                sums = [None] * templates
                for l in range(waves):
                    bright = power[l, pl.ds(pl.multiple_of(f * upix + first, step) + r, step), :]
                    spectrum = (bright * levels[l]).astype(jnp.bfloat16).astype(jnp.float32)
                    for j in range(templates):
                        term = spectrum * weights[pl.ds(f * templates + j, 1), l * PIX : (l + 1) * PIX]
                        sums[j] = term if l == 0 else sums[j] + term
                for j in range(templates):
                    store(j, r, sums[j].astype(jnp.bfloat16))
                return c

            lax.fori_loop(0, upix // 2 // step, chunk, 0)

        def to_partner(j, r, value):
            staged[f, j, pl.ds(r, step), :] = value

        def to_own(j, r, value):
            out_ref[side * fields + f, j, pl.ds(r, step), :] = value

        rows_of((1 - side) * (upix // 2), to_partner)
        out_copy(f).start()
        rows_of(side * (upix // 2), to_own)

    def tail(f, carry):
        last_units(f)

        @pl.when(f > 0)
        def _():
            mix_field(f - 1)

        last_images(f)
        return carry

    lax.fori_loop(0, fields, tail, 0)
    mix_field(fields - 1)
    for f in range(fields):
        out_landed(f).wait_recv()
        out_copy(f).wait_send()

    for d in range(1, slabs):
        length_copy(d, me).wait_send()
    for o in range(1, slabs):
        for c in range(CHUNKS):
            first_copy(o, c).wait_send()
            for e in range(1, chips):
                plane_copy(o, c, e).wait_send()
            core_copy(o, c, core).wait_send()


def local(sizes, waves, mode_basis, coef_table, table_index, wave_lengths, sed_table, template_ids):
    slabs, field_parts, group_parts = sizes
    count, rows, _ = mode_basis.shape
    fields, templates = template_ids.shape
    upix = 2 * PIX // slabs
    half = fields // 2
    chips = field_parts * group_parts // 2
    tiles = max(len(t) for t in packed_tiles(slabs, rows))
    share = -(-tiles * count // (2 * CHUNKS * chips))
    even = -(-tiles // BATCH) * BATCH
    units = max(share * 2 * CHUNKS * chips, even * count)

    hops = slabs - 1
    others = slabs // 2 - 1
    dma = pltpu.SemaphoreType.DMA

    return pl.pallas_call(
        functools.partial(psf_kernel, sizes, waves, half, share),
        in_specs=[
            pl.BlockSpec(memory_space=pltpu.VMEM),
            pl.BlockSpec(memory_space=pltpu.VMEM),
            pl.BlockSpec(memory_space=pltpu.SMEM),
            pl.BlockSpec(memory_space=pltpu.SMEM),
            pl.BlockSpec(memory_space=pltpu.SMEM),
            pl.BlockSpec(memory_space=pl.ANY),
        ],
        out_specs=pl.BlockSpec(memory_space=pltpu.VMEM),
        out_shape=jax.ShapeDtypeStruct((fields, templates, upix // 2, PIX), jnp.bfloat16),
        scratch_shapes=[
            pltpu.VMEM((half * GROUP, count * GROUP), jnp.bfloat16),
            pltpu.VMEM((half * templates, waves * PIX), jnp.float32),
            pltpu.VMEM((count, rows, PUP), jnp.bfloat16),
            pltpu.VMEM((slabs, units, GROUP, LANES), jnp.bfloat16),
            pltpu.VMEM((waves, 8, max(2 * rows, PIX)), jnp.float32),
            pltpu.VMEM((half, even, GROUP, LANES), jnp.float32),
            pltpu.VMEM((waves, half * upix, 2 * PUP), jnp.float32),
            pltpu.VMEM((waves if waves <= 8 else 1, 2 * PUP, 2 * PIX), jnp.bfloat16),
            pltpu.VMEM((waves, 2 * upix, 2 * rows), jnp.bfloat16),
            pltpu.VMEM((max(half, AHEAD), 2 * rows, PUP), jnp.bfloat16),
            pltpu.VMEM((rows, PUP), jnp.bfloat16),
            pltpu.VMEM((waves, half * upix, PIX), jnp.float32),
            pltpu.VMEM((half, waves, PIX), jnp.float32),
            pltpu.VMEM((others, half, waves, PIX), jnp.float32),
            pltpu.VMEM((half, templates, upix // 2, PIX), jnp.bfloat16),
            dma,
            dma((hops,)),
            dma((hops,)),
            dma((hops, CHUNKS)),
            dma((hops, CHUNKS)),
            dma((hops, CHUNKS, chips - 1)),
            dma((hops, CHUNKS, chips - 1)),
            dma((hops, CHUNKS)),
            dma((hops, CHUNKS)),
            dma((half, others)),
            dma((half, others)),
            dma((half,)),
            dma((half,)),
        ],
        compiler_params=pltpu.CompilerParams(
            vmem_limit_bytes=60 * 2**20, collective_id=0, has_side_effects=True
        ),
    )(coef_table.T, sed_table.T, table_index, template_ids, wave_lengths, mode_basis)


def solution(mesh):
    sizes = (mesh.shape["wave"], mesh.shape["field"], mesh.shape["groups"])


    def whole_program(*args):
        return sharded(mesh, functools.partial(local, sizes, args[3].shape[0]))(*args)

    return whole_program


def sharded(mesh, body):
    return jax.shard_map(
        body,
        mesh=mesh,
        in_specs=(
            P(None, "wave", None),
            P(),
            P(("groups", "field")),
            P("wave"),
            P(),
            P(("groups", "field"), None),
        ),
        out_specs=P(("groups", "field"), None, "wave", None),
        check_vma=False,
    )
```

```python
import functools

import jax
import jax.numpy as jnp
import numpy as np
from jax import lax
from jax.experimental import pallas as pl
from jax.experimental.pallas import tpu as pltpu
from jax.sharding import PartitionSpec as P

PUP = 512
PIX = 256
EPSILON = 1e-06
GROUP = 16
LANES = 128
CHUNKS = 2
AHEAD = 4
BATCH = 6
ROUNDER = 12582912.0

SIN = (4.442879676818848, -7.307816505432129, 3.5977742671966553, -0.7911993861198425)
COS = (1.4142135381698608, -6.978850841522217, 5.739460468292236, -1.883557915687561, 0.3106880187988281)
SHORT_SIN = (4.440917015075684, -7.256804466247559, 3.229630470275879)
SHORT_COS = (1.414183259010315, -6.976953506469727, 5.709674835205078, -1.7155721187591553)


def horner(coefficients, s):
    value = coefficients[-1]
    for c in coefficients[-2::-1]:
        value = c + s * value
    return value


def turns_sincos(turns, sine=SIN, cosine=COS):
    nearest = (turns + ROUNDER) - ROUNDER
    r = turns - nearest
    s = r * r
    a = r * horner(sine, s)
    b = horner(cosine, s)
    return 1.0 - a * a, a * b


def packed_tiles(slabs, rows):
    pos = 2 * np.arange(PUP) - PUP + 1
    radius = pos[:, None] ** 2 + pos[None, :] ** 2
    inside = (radius <= PUP * PUP) & (radius >= (61 * PUP // 100) ** 2)
    columns = PUP // LANES
    half = LANES // 2
    result = []
    for slab in range(slabs):
        tiles = []
        for group in range(rows // GROUP):
            first = slab * rows + group * GROUP
            need = inside[first : first + GROUP].any(axis=0).reshape(columns, LANES)
            low, high = need[:, :half].any(axis=1), need[:, half:].any(axis=1)
            lows = [c for c in range(columns) if low[c] and not high[c]]
            highs = [c for c in range(columns) if high[c] and not low[c]]
            pairs = list(zip(lows, highs))
            for c in range(columns):
                if low[c] and high[c]:
                    tiles.append((group, (c,)))
            tiles += [(group, pair) for pair in pairs]
            tiles += [(group, (c,)) for c in lows[len(pairs) :] + highs[len(pairs) :]]
        result.append(tuple(tiles))
    return result


def hop(order, slabs):
    odd = order % 2
    return odd * ((order + 1) // 2) + (1 - odd) * (slabs - order // 2)


def scheduled_events(slabs, waves):
    timed = []

    def add(block, eighth, *event):
        timed.append(((block * waves + eighth * waves // 8, eighth != 8, len(timed)), event))

    for o in range(1, slabs):
        if o == 1:
            for eighth, event in ((0, (1, 1, 0)), (1, (1, 1, 1)), (4, (2, 1, 0)), (6, (2, 1, 1)), (7, (3, 1, 0))):
                add(0, eighth, *event)
            if slabs > 2:
                add(0, 7, 1, 2, 0)
            add(0, 8, 3, 1, 1)
            if slabs > 2:
                add(0, 8, 1, 2, 1)
            add(0, 8, 0, 1, 0)
            add(0, 8, 4, 1, 0)
        elif o == 2:
            add(1, 0, 2, 2, 0)
            add(1, 2, 2, 2, 1)
            add(1, 2, 3, 2, 0)
            add(1, 6, 3, 2, 1)
            add(1, 8, 4, 2, 0)
        else:
            add(o - 2, 0, 1, o, 0)
            add(o - 2, 5, 1, o, 1)
            add(o - 2, 6, 2, o, 0)
            add(o - 1, 0, 2, o, 1)
            add(o - 1, 4, 3, o, 0)
            add(o - 1, 4, 3, o, 1)
            add(o - 1, 8, 4, o, 0)
    plan = {}
    for (step, *_), event in sorted(timed):
        plan.setdefault(step, []).append(event)
    return plan


def one_hot(targets, rows, columns):
    row = lax.broadcasted_iota(jnp.int32, (rows, columns), 0)
    wanted = jnp.zeros((rows, columns), jnp.int32)
    for i, target in enumerate(targets):
        wanted = jnp.where(row == i, target, wanted)
    column = lax.broadcasted_iota(jnp.int32, (rows, columns), 1)
    return (column == wanted).astype(jnp.float32).astype(jnp.bfloat16)


def same_place(shape, row_shift, column_shift, row_mask=-1, column_mask=-1):
    row = (lax.broadcasted_iota(jnp.int32, shape, 0) >> row_shift) & row_mask
    column = (lax.broadcasted_iota(jnp.int32, shape, 1) >> column_shift) & column_mask
    return (row == column).astype(jnp.float32)


def last_with_last(a, b):
    return lax.dot_general(a, b, (((1,), (1,)), ((), ())), preferred_element_type=jnp.float32)


def gather_parameters(side, fields, templates, waves, count, coef_ref, sed_ref, index_ref, ids_ref, mix, weights):
    bf16 = jnp.bfloat16
    wanted = one_hot([index_ref[side * fields + f] for f in range(fields)], 8 * -(-fields // 8), coef_ref.shape[1])
    coeffs = last_with_last(wanted, coef_ref[...])[:fields].astype(bf16)
    bits = GROUP.bit_length() - 1
    tall = same_place((fields * GROUP, fields), bits, 0).astype(bf16)
    wide = same_place((count, count * GROUP), 0, bits).astype(bf16)
    spread = jnp.dot(tall, coeffs, preferred_element_type=jnp.float32).astype(bf16)
    spread = jnp.dot(spread, wide, preferred_element_type=jnp.float32)
    mix[...] = (spread * same_place(spread.shape, 0, 0, GROUP - 1, GROUP - 1)).astype(bf16)

    ids = [ids_ref[f, j] for f in range(2 * fields) for j in range(templates)]
    wanted = one_hot(ids, 2 * fields * templates, sed_ref.shape[1])
    table = sed_ref[...]
    high = table.astype(bf16)
    middle = (table - high.astype(jnp.float32)).astype(bf16)
    low = (table - high.astype(jnp.float32) - middle.astype(jnp.float32)).astype(bf16)
    raw = last_with_last(wanted, high) + last_with_last(wanted, middle) + last_with_last(wanted, low)
    shares = (raw / jnp.sum(raw, axis=1, keepdims=True)).astype(bf16)
    bits = PIX.bit_length() - 1
    weights[...] = jnp.dot(shares, same_place((waves, waves * PIX), 0, bits).astype(bf16), preferred_element_type=jnp.float32)


def psf_kernel(
    sizes, waves, fields, share, coef_ref, sed_ref, index_ref, ids_ref, length_ref, basis_ref, out_ref,
    mix, weights, held, whole, inverse, path, image, tables, xtables, efields, opening, power, total, arrived, incoming,
    local_sem, wl_send, wl_recv, send1, recv1, send2, recv2, send3, recv3, sum_send, sum_recv, out_send, out_recv,
):
    slabs, field_parts, group_parts = sizes
    count, rows, _ = basis_ref.shape
    upix = 2 * PIX // slabs
    own_waves = waves // slabs
    x_parts = field_parts // 2
    chips = x_parts * group_parts
    templates = out_ref.shape[1]
    layout = packed_tiles(slabs, rows)
    kept_tables = tables.shape[0] == waves

    me = lax.axis_index("wave")
    part = lax.axis_index("field")
    core = part % 2
    chip = lax.axis_index("groups") * x_parts + part // 2
    side = me % 2
    first_pix = (me // 2) * upix
    partner = {"wave": me + 1 - 2 * side}

    def wave_peer(shift):
        return {"wave": (me + shift) % slabs}

    def chip_device(other):
        return {"groups": other // x_parts, "field": (other % x_parts) * 2 + core}

    sibling = {"field": part + 1 - 2 * core}

    def remote(src, dst, send, recv, device):
        return pltpu.make_async_remote_copy(
            src_ref=src, dst_ref=dst, send_sem=send, recv_sem=recv,
            device_id=device, device_id_type=pl.DeviceIdType.MESH,
        )

    def from_slab(order):
        return (me + 2 * slabs - hop(order, slabs)) % slabs

    def block(slab, of_core, chunk, of_chip, pieces=1):
        first = ((of_core * CHUNKS + chunk) * chips + of_chip) * share
        return whole.at[slab, pl.ds(first, pieces * share)]

    def first_copy(order, chunk):
        ref = block(me, core, chunk, chip)
        at = (order - 1, chunk)
        return remote(ref, ref, send1.at[at], recv1.at[at], wave_peer(hop(order, slabs)))

    def first_landed(order, chunk):
        ref = block(from_slab(order), core, chunk, chip)
        at = (order - 1, chunk)
        return remote(ref, ref, send1.at[at], recv1.at[at], wave_peer(hop(order, slabs)))

    relay = x_parts == 2 and group_parts == 2
    chip_x, chip_y = chip % x_parts, chip // x_parts
    flip_x, flip_y = 1 - 2 * chip_x, 1 - 2 * chip_y
    first_chip = (chip_y + core * flip_y) * x_parts + chip_x + (1 - core) * flip_x
    second_chip = (chip_y + (1 - core) * flip_y) * x_parts + chip_x + core * flip_x

    def plane_copy(order, chunk, shift):
        at = (order - 1, chunk, shift - 1)
        slab = from_slab(order)
        if relay:
            ref = block(slab, core, chunk, first_chip if shift == 3 else chip)
            device = chip_device(first_chip if shift == 1 else second_chip)
        else:
            ref = block(slab, core, chunk, chip)
            device = chip_device((chip + shift) % chips)
        return remote(ref, ref, send2.at[at], recv2.at[at], device)

    def plane_landed(order, chunk, shift):
        at = (order - 1, chunk, shift - 1)
        if relay:
            sender = (first_chip, second_chip, chips - 1 - chip)[shift - 1]
        else:
            sender = (chip + chips - shift) % chips
        ref = block(from_slab(order), core, chunk, sender)
        return remote(ref, ref, send2.at[at], recv2.at[at], chip_device((chip + shift) % chips))

    def core_copy(order, chunk, which):
        ref = block(from_slab(order), which, chunk, 0, chips)
        at = (order - 1, chunk)
        return remote(ref, ref, send3.at[at], recv3.at[at], sibling)

    def length_copy(shift, sender):
        ref = inverse.at[pl.ds(sender * own_waves, own_waves)]
        return remote(ref, ref, wl_send.at[shift - 1], wl_recv.at[shift - 1], wave_peer(shift))

    barrier = pltpu.get_barrier_semaphore()
    peers = [wave_peer(d) for d in range(1, slabs)] + [chip_device((chip + e) % chips) for e in range(1, chips)] + [sibling]
    for peer in peers:
        pl.semaphore_signal(barrier, inc=1, device_id=peer, device_id_type=pl.DeviceIdType.MESH)
    bring = pltpu.make_async_copy(basis_ref, held, local_sem)
    bring.start()
    for i in range(own_waves):
        inverse[me * own_waves + i] = 1.0 / jnp.full(inverse.shape[1:], length_ref[i], jnp.float32)

    def clear(f, carry):
        for l in range(waves):
            image[l, pl.ds(f * upix, upix), :] = jnp.zeros((upix, 2 * PUP), jnp.float32)
        return carry

    bring.wait()

    low_lanes = (lax.broadcasted_iota(jnp.int32, (GROUP, LANES), 1) < LANES // 2).astype(jnp.float32)
    low_lanes, high_lanes = low_lanes.astype(jnp.bfloat16), (1.0 - low_lanes).astype(jnp.bfloat16)

    def pack(tiles, k, carry):
        for t, (group, columns) in enumerate(tiles):
            r = group * GROUP
            parts = [held[k, r : r + GROUP, c * LANES : (c + 1) * LANES] for c in columns]
            value = parts[0]
            if len(parts) == 2:
                value = parts[0] * low_lanes + parts[1] * high_lanes
            whole[me, t * count + k] = value
        return carry

    for slab, tiles in enumerate(layout):

        @pl.when(me == slab)
        def _():
            lax.fori_loop(0, count, functools.partial(pack, tiles), 0)

    pl.semaphore_wait(barrier, len(peers))
    for c in range(CHUNKS):
        first_copy(1, c).start()
    for d in range(1, slabs):
        length_copy(d, me).start()
    gather_parameters(side, fields, templates, waves, count, coef_ref, sed_ref, index_ref, ids_ref, mix, weights)
    lax.fori_loop(0, fields, clear, 0)
    for d in range(1, slabs):
        length_copy(d, (me + slabs - d) % slabs).wait_recv()

    def second_table(wave, slot):
        scale = inverse[wave][:1, :PIX] * (0.25 / (2.0 * PUP))
        step = 64
        for r in range(0, PUP, step):
            ys = 2 * (r + lax.broadcasted_iota(jnp.int32, (step, PIX), 0)) - PUP + 1
            vs = lax.broadcasted_iota(jnp.int32, (step, PIX), 1) - PIX // 2
            cosine, sine = turns_sincos((ys * vs).astype(jnp.float32) * scale)
            cosine = cosine.astype(jnp.bfloat16)
            tables[slot, r : r + step, :PIX] = cosine
            tables[slot, r : r + step, PIX:] = (-sine).astype(jnp.bfloat16)
            tables[slot, PUP + r : PUP + r + step, :PIX] = sine.astype(jnp.bfloat16)
            tables[slot, PUP + r : PUP + r + step, PIX:] = cosine

    def x_table(slab, wave):
        xs = 2 * (slab * rows + lax.broadcasted_iota(jnp.int32, (upix, rows), 1)) - PUP + 1
        us = first_pix + lax.broadcasted_iota(jnp.int32, (upix, rows), 0) - PIX // 2
        scale = inverse[wave][:1, :rows] * (0.25 / (2.0 * PUP))
        cosine, sine = turns_sincos((us * xs).astype(jnp.float32) * scale)
        upper = jnp.concatenate([cosine, sine], axis=1)
        lower = jnp.concatenate([-sine, cosine], axis=1)
        return jnp.concatenate([upper, lower], axis=0).astype(jnp.bfloat16)

    def open_slab(slab):
        def openings(g, c):
            r = pl.multiple_of(g * GROUP, GROUP)
            x = 2 * (slab * rows + r + lax.broadcasted_iota(jnp.int32, (GROUP, PUP), 0)) - PUP + 1
            y = 2 * lax.broadcasted_iota(jnp.int32, (GROUP, PUP), 1) - PUP + 1
            radius = x * x + y * y
            inner = 61 * PUP // 100
            inside = (radius <= PUP * PUP) & (radius >= inner * inner)
            opening[pl.ds(r, GROUP), :] = inside.astype(jnp.float32).astype(jnp.bfloat16)
            return c

        lax.fori_loop(0, rows // GROUP, openings, 0)
        for i in range(efields.shape[0]):
            efields[i] = jnp.zeros(efields.shape[1:], efields.dtype)

    def slab_paths(slab):
        def paths(i, c):
            for q in range(BATCH // 2):
                first = BATCH * i + 2 * q
                pair = [whole[slab, pl.ds((first + b) * count, count)].reshape(count * GROUP, LANES) for b in range(2)]
                diff = jnp.dot(mix[...], jnp.concatenate(pair, axis=1), preferred_element_type=jnp.float32)
                for b in range(2):
                    path[:, first + b] = diff[:, b * LANES : (b + 1) * LANES].reshape(fields, GROUP, LANES)
            return c

        batches = 0
        for number, tiles in enumerate(layout):
            batches = jnp.where(slab == number, -(-len(tiles) // BATCH), batches)
        lax.fori_loop(0, batches, paths, 0)

    def fill(field, tiles, f, inv):
        for t, (group, columns) in enumerate(tiles):
            r = group * GROUP
            cosine, sine = turns_sincos(path[f, t] * inv, SHORT_SIN, SHORT_COS)
            cosine, sine = cosine.astype(jnp.bfloat16), sine.astype(jnp.bfloat16)
            for c in columns:
                lanes = slice(c * LANES, (c + 1) * LANES)
                hole = opening[r : r + GROUP, lanes]
                efields[field, r : r + GROUP, lanes] = cosine * hole
                efields[field, rows + r : rows + r + GROUP, lanes] = sine * hole

    def inverse_tile(wave):
        inv = inverse[wave]
        return jnp.concatenate([inv[:, :LANES], inv[:, :LANES]], axis=0)

    def accumulate(kernel, field, wave, f):
        part_sum = jnp.dot(kernel, efields[field], preferred_element_type=jnp.float32)
        here = pl.ds(f * upix, upix)
        image[wave, here, :PUP] += part_sum[:upix]
        image[wave, here, PUP:] += part_sum[upix:]

    def handle(event):
        stage, o, c = event
        if stage == 0 and kept_tables:
            def make(l, carry):
                second_table(l, l)
                return carry

            lax.fori_loop(0, waves, make, 0)
        if stage == 1:
            first_landed(o, c).wait_recv()
            for e in range(1, 3 if relay else chips):
                plane_copy(o, c, e).start()
            if o + 1 < slabs:
                first_copy(o + 1, c).start()
        if stage == 2 and relay:
            plane_landed(o, c, 1).wait_recv()
            plane_copy(o, c, 3).start()
        if stage == 3:
            for e in range(2 if relay else 1, chips):
                plane_landed(o, c, e).wait_recv()
            core_copy(o, c, core).start()
        if stage == 4:
            for each in range(CHUNKS):
                core_copy(o, each, 1 - core).wait_recv()

    plan = scheduled_events(slabs, waves)
    last_step = (slabs - 1) * waves

    def step_body(step, carry):
        order = step // waves
        wave = step % waves
        slab = from_slab(order)

        for at, events in plan.items():
            if at < last_step:

                @pl.when(step == at)
                def _():
                    for event in events:
                        handle(event)

        @pl.when(wave == 0)
        def _():
            slab_paths(slab)
            open_slab(slab)

        kernel = x_table(slab, wave)
        inv = inverse_tile(wave)

        def units(tiles):
            for f in range(fields):
                fill(f, tiles, f, inv)
            for f in range(fields):
                accumulate(kernel, f, wave, f)

        for number, tiles in enumerate(layout):
            pl.when(slab == number)(functools.partial(units, tiles))

        return carry

    lax.fori_loop(0, last_step, step_body, 0)

    last = from_slab(slabs - 1)

    def make_x(l, c):
        xtables[l] = x_table(last, l)
        return c

    lax.fori_loop(0, waves, make_x, 0)
    open_slab(last)
    for event in plan[last_step]:
        handle(event)
    slab_paths(last)

    def sum_copy(f, shift):
        at = (f, shift - 1)
        return remote(total.at[f], arrived.at[shift - 1, f], sum_send.at[at], sum_recv.at[at], wave_peer(shift))

    def exchange(f):
        return remote(power.at[f, 1 - side], incoming.at[f], out_send.at[f], out_recv.at[f], partner)

    def last_units(f):
        def some_waves(i, c):
            def units(tiles):
                for b in range(AHEAD):
                    fill(b, tiles, f, inverse_tile(AHEAD * i + b))
                for b in range(AHEAD):
                    accumulate(xtables[AHEAD * i + b], b, AHEAD * i + b, f)

            for number, tiles in enumerate(layout):
                pl.when(last == number)(functools.partial(units, tiles))
            return c

        lax.fori_loop(0, waves // AHEAD, some_waves, 0)

    def last_images(f):
        here = pl.ds(pl.multiple_of(f * upix, GROUP), upix)

        def finish(i, c):
            for b in range(AHEAD):
                wave = AHEAD * i + b
                if not kept_tables:
                    second_table(wave, 0)
                field = jnp.dot(
                    image[wave, here, :].astype(jnp.bfloat16),
                    tables[wave if kept_tables else 0],
                    preferred_element_type=jnp.float32,
                )
                re, im = field[:, :PIX], field[:, PIX:]
                bright = re * re + im * im
                for h in range(2):
                    power[f, h, wave] = bright[h * upix // 2 : (h + 1) * upix // 2].astype(jnp.bfloat16)
                total[f, pl.ds(wave, 1), :] = jnp.sum(bright, axis=0, keepdims=True)
            return c

        lax.fori_loop(0, waves // AHEAD, finish, 0)
        total[f] = jnp.broadcast_to(jnp.sum(total[f], axis=1, keepdims=True), (waves, PIX))
        for d in range(1, slabs):
            sum_copy(f, d).start()
        exchange(f).start()

    def mix_field(field, everything, source):
        level_all = 1.0 / (everything * (1.0 / (PIX * PIX)) + EPSILON)
        levels = [level_all[l : l + 1, :] for l in range(waves)]
        step = 16

        def chunk(i, c):
            r = pl.multiple_of(i * step, step)
            sums = [None] * templates
            for l in range(waves):
                spectrum = source[l, pl.ds(r, step), :].astype(jnp.float32) * levels[l]
                for j in range(templates):
                    term = spectrum * weights[pl.ds(field * templates + j, 1), l * PIX : (l + 1) * PIX]
                    sums[j] = term if l == 0 else sums[j] + term
            for j in range(templates):
                out_ref[field, j, pl.ds(r, step), :] = sums[j].astype(jnp.bfloat16)
            return c

        lax.fori_loop(0, upix // 2 // step, chunk, 0)

    def mix_own(f):
        everything = total[f]
        for d in range(2, slabs, 2):
            sum_copy(f, d).wait()
            everything = everything + arrived[d - 1, f]
        mix_field(side * fields + f, everything, power.at[f, side])

    def mix_other(f):
        everything = None
        for d in range(1, slabs, 2):
            sum_copy(f, d).wait()
            everything = arrived[d - 1, f] if d == 1 else everything + arrived[d - 1, f]
        exchange(f).wait()
        mix_field((1 - side) * fields + f, everything, incoming.at[f])

    def tail(f, carry):
        last_units(f)

        @pl.when(f > 0)
        def _():
            mix_own(f - 1)

        @pl.when(f > 1)
        def _():
            mix_other(f - 2)

        last_images(f)
        return carry

    lax.fori_loop(0, fields, tail, 0)
    mix_own(fields - 1)
    for f in range(max(fields - 2, 0), fields):
        mix_other(f)

    for d in range(1, slabs):
        length_copy(d, me).wait_send()
    for o in range(1, slabs):
        for c in range(CHUNKS):
            first_copy(o, c).wait_send()
            for e in range(1, chips):
                plane_copy(o, c, e).wait_send()
            core_copy(o, c, core).wait_send()


def local(sizes, waves, mode_basis, coef_table, table_index, wave_lengths, sed_table, template_ids):
    slabs, field_parts, group_parts = sizes
    count, rows, _ = mode_basis.shape
    fields, templates = template_ids.shape
    upix = 2 * PIX // slabs
    half = fields // 2
    chips = field_parts * group_parts // 2
    tiles = max(len(t) for t in packed_tiles(slabs, rows))
    share = -(-tiles * count // (2 * CHUNKS * chips))
    even = -(-tiles // BATCH) * BATCH
    units = max(share * 2 * CHUNKS * chips, even * count)

    hops = slabs - 1
    dma = pltpu.SemaphoreType.DMA

    return pl.pallas_call(
        functools.partial(psf_kernel, sizes, waves, half, share),
        in_specs=[
            pl.BlockSpec(memory_space=pltpu.VMEM),
            pl.BlockSpec(memory_space=pltpu.VMEM),
            pl.BlockSpec(memory_space=pltpu.SMEM),
            pl.BlockSpec(memory_space=pltpu.SMEM),
            pl.BlockSpec(memory_space=pltpu.SMEM),
            pl.BlockSpec(memory_space=pl.ANY),
        ],
        out_specs=pl.BlockSpec(memory_space=pltpu.VMEM),
        out_shape=jax.ShapeDtypeStruct((fields, templates, upix // 2, PIX), jnp.bfloat16),
        scratch_shapes=[
            pltpu.VMEM((half * GROUP, count * GROUP), jnp.bfloat16),
            pltpu.VMEM((fields * templates, waves * PIX), jnp.float32),
            pltpu.VMEM((count, rows, PUP), jnp.bfloat16),
            pltpu.VMEM((slabs, units, GROUP, LANES), jnp.bfloat16),
            pltpu.VMEM((waves, 8, max(2 * rows, PIX)), jnp.float32),
            pltpu.VMEM((half, even, GROUP, LANES), jnp.float32),
            pltpu.VMEM((waves, half * upix, 2 * PUP), jnp.float32),
            pltpu.VMEM((waves if waves <= 8 else 1, 2 * PUP, 2 * PIX), jnp.bfloat16),
            pltpu.VMEM((waves, 2 * upix, 2 * rows), jnp.bfloat16),
            pltpu.VMEM((max(half, AHEAD), 2 * rows, PUP), jnp.bfloat16),
            pltpu.VMEM((rows, PUP), jnp.bfloat16),
            pltpu.VMEM((half, 2, waves, upix // 2, PIX), jnp.bfloat16),
            pltpu.VMEM((half, waves, PIX), jnp.float32),
            pltpu.VMEM((hops, half, waves, PIX), jnp.float32),
            pltpu.VMEM((half, waves, upix // 2, PIX), jnp.bfloat16),
            dma,
            dma((hops,)),
            dma((hops,)),
            dma((hops, CHUNKS)),
            dma((hops, CHUNKS)),
            dma((hops, CHUNKS, chips - 1)),
            dma((hops, CHUNKS, chips - 1)),
            dma((hops, CHUNKS)),
            dma((hops, CHUNKS)),
            dma((half, hops)),
            dma((half, hops)),
            dma((half,)),
            dma((half,)),
        ],
        compiler_params=pltpu.CompilerParams(
            vmem_limit_bytes=60 * 2**20, collective_id=0, has_side_effects=True
        ),
    )(coef_table.T, sed_table.T, table_index, template_ids, wave_lengths, mode_basis)


def solution(mesh):
    sizes = (mesh.shape["wave"], mesh.shape["field"], mesh.shape["groups"])


    def whole_program(*args):
        return sharded(mesh, functools.partial(local, sizes, args[3].shape[0]))(*args)

    return whole_program


def sharded(mesh, body):
    return jax.shard_map(
        body,
        mesh=mesh,
        in_specs=(
            P(None, "wave", None),
            P(),
            P(("groups", "field")),
            P("wave"),
            P(),
            P(("groups", "field"), None),
        ),
        out_specs=P(("groups", "field"), None, "wave", None),
        check_vma=False,
    )
```

```python
import functools

import jax
import jax.numpy as jnp
import numpy as np
from jax import lax
from jax.experimental import pallas as pl
from jax.experimental.pallas import tpu as pltpu
from jax.sharding import PartitionSpec as P

PUP = 512
PIX = 256
EPSILON = 1e-06
GROUP = 16
LANES = 128
CHUNKS = 2
AHEAD = 4
BATCH = 6
LIMIT = 54
ROUNDER = 12582912.0

SIN = (4.442879676818848, -7.307816505432129, 3.5977742671966553, -0.7911993861198425)
COS = (1.4142135381698608, -6.978850841522217, 5.739460468292236, -1.883557915687561, 0.3106880187988281)
SHORT_SIN = (4.440917015075684, -7.256804466247559, 3.229630470275879)
SHORT_COS = (1.4140625, -6.96875, 5.65625, -1.7265625)


def horner(coefficients, s):
    value = coefficients[-1]
    for c in coefficients[-2::-1]:
        value = c + s * value
    return value


def turns_sincos(turns, sine=SIN, cosine=COS):
    nearest = (turns + ROUNDER) - ROUNDER
    r = turns - nearest
    s = r * r
    a = r * horner(sine, s)
    b = horner(cosine, s)
    return 1.0 - a * a, a * b


def rounded_sincos(turns):
    nearest = (turns + ROUNDER) - ROUNDER
    r = turns - nearest
    s = r * r
    a = r * horner(SHORT_SIN, s)
    b = horner([jnp.bfloat16(c) for c in SHORT_COS], s.astype(jnp.bfloat16))
    return (1.0 - a * a).astype(jnp.bfloat16), a.astype(jnp.bfloat16) * b


def packed_tiles(slabs, rows):
    pos = 2 * np.arange(PUP) - PUP + 1
    radius = pos[:, None] ** 2 + pos[None, :] ** 2
    inside = (radius <= PUP * PUP) & (radius >= (61 * PUP // 100) ** 2)
    columns = PUP // LANES
    half = LANES // 2
    result = []
    for slab in range(slabs):
        tiles = []
        for group in range(rows // GROUP):
            first = slab * rows + group * GROUP
            need = inside[first : first + GROUP].any(axis=0).reshape(columns, LANES)
            low, high = need[:, :half].any(axis=1), need[:, half:].any(axis=1)
            lows = [c for c in range(columns) if low[c] and not high[c]]
            highs = [c for c in range(columns) if high[c] and not low[c]]
            pairs = list(zip(lows, highs))
            for c in range(columns):
                if low[c] and high[c]:
                    tiles.append((group, (c,)))
            tiles += [(group, pair) for pair in pairs]
            tiles += [(group, (c,)) for c in lows[len(pairs) :] + highs[len(pairs) :]]
        result.append(tuple(tiles))
    return result


def hop(order, slabs):
    odd = order % 2
    return odd * ((order + 1) // 2) + (1 - odd) * (slabs - order // 2)


def scheduled_events(slabs, waves):
    timed = []

    def add(block, eighth, *event):
        timed.append(((block * waves + eighth * waves // 8, eighth != 8, len(timed)), event))

    for o in range(1, slabs):
        if o == 1:
            for eighth, event in ((0, (1, 1, 0)), (1, (1, 1, 1)), (4, (2, 1, 0)), (6, (2, 1, 1)), (7, (3, 1, 0))):
                add(0, eighth, *event)
            if slabs > 2:
                add(0, 7, 1, 2, 0)
            add(0, 8, 3, 1, 1)
            if slabs > 2:
                add(0, 8, 1, 2, 1)
            add(0, 8, 0, 1, 0)
            add(0, 8, 4, 1, 0)
        elif o == 2:
            add(1, 0, 2, 2, 0)
            add(1, 2, 2, 2, 1)
            add(1, 2, 3, 2, 0)
            add(1, 6, 3, 2, 1)
            add(1, 8, 4, 2, 0)
        else:
            add(o - 2, 0, 1, o, 0)
            add(o - 2, 5, 1, o, 1)
            add(o - 2, 6, 2, o, 0)
            add(o - 1, 0, 2, o, 1)
            add(o - 1, 4, 3, o, 0)
            add(o - 1, 4, 3, o, 1)
            add(o - 1, 8, 4, o, 0)
    plan = {}
    for (step, *_), event in sorted(timed):
        plan.setdefault(step, []).append(event)
    return plan


def one_hot(targets, rows, columns):
    row = lax.broadcasted_iota(jnp.int32, (rows, columns), 0)
    wanted = jnp.zeros((rows, columns), jnp.int32)
    for i, target in enumerate(targets):
        wanted = jnp.where(row == i, target, wanted)
    column = lax.broadcasted_iota(jnp.int32, (rows, columns), 1)
    return (column == wanted).astype(jnp.float32).astype(jnp.bfloat16)


def same_place(shape, row_shift, column_shift, row_mask=-1, column_mask=-1):
    row = (lax.broadcasted_iota(jnp.int32, shape, 0) >> row_shift) & row_mask
    column = (lax.broadcasted_iota(jnp.int32, shape, 1) >> column_shift) & column_mask
    return (row == column).astype(jnp.float32)


def last_with_last(a, b):
    return lax.dot_general(a, b, (((1,), (1,)), ((), ())), preferred_element_type=jnp.float32)


def gather_parameters(side, fields, templates, waves, count, coef_ref, sed_ref, index_ref, ids_ref, mix, weights):
    bf16 = jnp.bfloat16
    wanted = one_hot([index_ref[side * fields + f] for f in range(fields)], 8 * -(-fields // 8), coef_ref.shape[1])
    coeffs = last_with_last(wanted, coef_ref[...])[:fields].astype(bf16)
    bits = GROUP.bit_length() - 1
    tall = same_place((fields * GROUP, fields), bits, 0).astype(bf16)
    wide = same_place((count, count * GROUP), 0, bits).astype(bf16)
    spread = jnp.dot(tall, coeffs, preferred_element_type=jnp.float32).astype(bf16)
    spread = jnp.dot(spread, wide, preferred_element_type=jnp.float32)
    mix[...] = (spread * same_place(spread.shape, 0, 0, GROUP - 1, GROUP - 1)).astype(bf16)

    ids = [ids_ref[f, j] for f in range(2 * fields) for j in range(templates)]
    wanted = one_hot(ids, 2 * fields * templates, sed_ref.shape[1])
    table = sed_ref[...]
    high = table.astype(bf16)
    middle = (table - high.astype(jnp.float32)).astype(bf16)
    low = (table - high.astype(jnp.float32) - middle.astype(jnp.float32)).astype(bf16)
    raw = last_with_last(wanted, high) + last_with_last(wanted, middle) + last_with_last(wanted, low)
    shares = (raw / jnp.sum(raw, axis=1, keepdims=True)).astype(bf16)
    bits = PIX.bit_length() - 1
    weights[...] = jnp.dot(shares, same_place((waves, waves * PIX), 0, bits).astype(bf16), preferred_element_type=jnp.float32)


def psf_kernel(
    sizes, waves, fields, share, coef_ref, sed_ref, index_ref, ids_ref, length_ref, basis_ref, out_ref,
    mix, weights, held, whole, inverse, path, image, tables, xtables, efields, opening, power, total, arrived, incoming, mixed,
    local_sem, wl_send, wl_recv, send1, recv1, send2, recv2, send3, recv3, sum_send, sum_recv, out_send, out_recv, result_sem,
):
    slabs, field_parts, group_parts = sizes
    count, rows, _ = basis_ref.shape
    upix = 2 * PIX // slabs
    own_waves = waves // slabs
    x_parts = field_parts // 2
    chips = x_parts * group_parts
    templates = out_ref.shape[1]
    layout = packed_tiles(slabs, rows)
    kept_tables = tables.shape[0] == waves

    me = lax.axis_index("wave")
    part = lax.axis_index("field")
    core = part % 2
    chip = lax.axis_index("groups") * x_parts + part // 2
    side = me % 2
    first_pix = (me // 2) * upix
    partner = {"wave": me + 1 - 2 * side}

    def wave_peer(shift):
        return {"wave": (me + shift) % slabs}

    def chip_device(other):
        return {"groups": other // x_parts, "field": (other % x_parts) * 2 + core}

    sibling = {"field": part + 1 - 2 * core}

    def remote(src, dst, send, recv, device):
        return pltpu.make_async_remote_copy(
            src_ref=src, dst_ref=dst, send_sem=send, recv_sem=recv,
            device_id=device, device_id_type=pl.DeviceIdType.MESH,
        )

    def from_slab(order):
        return (me + 2 * slabs - hop(order, slabs)) % slabs

    def block(slab, of_core, chunk, of_chip, pieces=1):
        first = ((of_core * CHUNKS + chunk) * chips + of_chip) * share
        return whole.at[slab, pl.ds(first, pieces * share)]

    def first_copy(order, chunk):
        ref = block(me, core, chunk, chip)
        at = (order - 1, chunk)
        return remote(ref, ref, send1.at[at], recv1.at[at], wave_peer(hop(order, slabs)))

    def first_landed(order, chunk):
        ref = block(from_slab(order), core, chunk, chip)
        at = (order - 1, chunk)
        return remote(ref, ref, send1.at[at], recv1.at[at], wave_peer(hop(order, slabs)))

    relay = x_parts == 2 and group_parts == 2
    chip_x, chip_y = chip % x_parts, chip // x_parts
    flip_x, flip_y = 1 - 2 * chip_x, 1 - 2 * chip_y
    first_chip = (chip_y + core * flip_y) * x_parts + chip_x + (1 - core) * flip_x
    second_chip = (chip_y + (1 - core) * flip_y) * x_parts + chip_x + core * flip_x

    def plane_copy(order, chunk, shift):
        at = (order - 1, chunk, shift - 1)
        slab = from_slab(order)
        if relay:
            ref = block(slab, core, chunk, first_chip if shift == 3 else chip)
            device = chip_device(first_chip if shift == 1 else second_chip)
        else:
            ref = block(slab, core, chunk, chip)
            device = chip_device((chip + shift) % chips)
        return remote(ref, ref, send2.at[at], recv2.at[at], device)

    def plane_landed(order, chunk, shift):
        at = (order - 1, chunk, shift - 1)
        if relay:
            sender = (first_chip, second_chip, chips - 1 - chip)[shift - 1]
        else:
            sender = (chip + chips - shift) % chips
        ref = block(from_slab(order), core, chunk, sender)
        return remote(ref, ref, send2.at[at], recv2.at[at], chip_device((chip + shift) % chips))

    def core_copy(order, chunk, which):
        ref = block(from_slab(order), which, chunk, 0, chips)
        at = (order - 1, chunk)
        return remote(ref, ref, send3.at[at], recv3.at[at], sibling)

    def length_copy(shift, sender):
        ref = inverse.at[pl.ds(sender * own_waves, own_waves)]
        return remote(ref, ref, wl_send.at[shift - 1], wl_recv.at[shift - 1], wave_peer(shift))

    barrier = pltpu.get_barrier_semaphore()
    peers = [wave_peer(d) for d in range(1, slabs)] + [chip_device((chip + e) % chips) for e in range(1, chips)] + [sibling]
    for peer in peers:
        pl.semaphore_signal(barrier, inc=1, device_id=peer, device_id_type=pl.DeviceIdType.MESH)
    bring = pltpu.make_async_copy(basis_ref, held, local_sem)
    bring.start()
    for i in range(own_waves):
        inverse[me * own_waves + i] = 1.0 / jnp.full(inverse.shape[1:], length_ref[i], jnp.float32)

    def clear(f, carry):
        for l in range(waves):
            image[l, pl.ds(f * upix, upix), :] = jnp.zeros((upix, 2 * PUP), jnp.float32)
        return carry

    bring.wait()

    low_lanes = (lax.broadcasted_iota(jnp.int32, (GROUP, LANES), 1) < LANES // 2).astype(jnp.float32)
    low_lanes, high_lanes = low_lanes.astype(jnp.bfloat16), (1.0 - low_lanes).astype(jnp.bfloat16)

    def pack(tiles, k, carry):
        for t, (group, columns) in enumerate(tiles):
            r = group * GROUP
            parts = [held[k, r : r + GROUP, c * LANES : (c + 1) * LANES] for c in columns]
            value = parts[0]
            if len(parts) == 2:
                value = parts[0] * low_lanes + parts[1] * high_lanes
            whole[me, t * count + k] = value
        return carry

    for slab, tiles in enumerate(layout):

        @pl.when(me == slab)
        def _():
            lax.fori_loop(0, count, functools.partial(pack, tiles), 0)

    pl.semaphore_wait(barrier, len(peers))
    for c in range(CHUNKS):
        first_copy(1, c).start()
    for d in range(1, slabs):
        length_copy(d, me).start()
    gather_parameters(side, fields, templates, waves, count, coef_ref, sed_ref, index_ref, ids_ref, mix, weights)
    lax.fori_loop(0, fields, clear, 0)
    for d in range(1, slabs):
        length_copy(d, (me + slabs - d) % slabs).wait_recv()

    def second_table(wave, slot):
        scale = inverse[wave][:1, :PIX] * (0.25 / (2.0 * PUP))
        step = 64
        for r in range(0, PUP, step):
            ys = 2 * (r + lax.broadcasted_iota(jnp.int32, (step, PIX), 0)) - PUP + 1
            vs = lax.broadcasted_iota(jnp.int32, (step, PIX), 1) - PIX // 2
            cosine, sine = turns_sincos((ys * vs).astype(jnp.float32) * scale)
            cosine = cosine.astype(jnp.bfloat16)
            tables[slot, r : r + step, :PIX] = cosine
            tables[slot, r : r + step, PIX:] = (-sine).astype(jnp.bfloat16)
            tables[slot, PUP + r : PUP + r + step, :PIX] = sine.astype(jnp.bfloat16)
            tables[slot, PUP + r : PUP + r + step, PIX:] = cosine

    def x_table(slab, wave):
        xs = 2 * (slab * rows + lax.broadcasted_iota(jnp.int32, (upix, rows), 1)) - PUP + 1
        us = first_pix + lax.broadcasted_iota(jnp.int32, (upix, rows), 0) - PIX // 2
        scale = inverse[wave][:1, :rows] * (0.25 / (2.0 * PUP))
        cosine, sine = turns_sincos((us * xs).astype(jnp.float32) * scale)
        upper = jnp.concatenate([cosine, sine], axis=1)
        lower = jnp.concatenate([-sine, cosine], axis=1)
        return jnp.concatenate([upper, lower], axis=0).astype(jnp.bfloat16)

    def open_slab(slab):
        def openings(g, c):
            r = pl.multiple_of(g * GROUP, GROUP)
            x = 2 * (slab * rows + r + lax.broadcasted_iota(jnp.int32, (GROUP, PUP), 0)) - PUP + 1
            y = 2 * lax.broadcasted_iota(jnp.int32, (GROUP, PUP), 1) - PUP + 1
            radius = x * x + y * y
            inner = 61 * PUP // 100
            inside = (radius <= PUP * PUP) & (radius >= inner * inner)
            opening[pl.ds(r, GROUP), :] = inside.astype(jnp.float32).astype(jnp.bfloat16)
            return c

        lax.fori_loop(0, rows // GROUP, openings, 0)
        for i in range(efields.shape[0]):
            efields[i] = jnp.zeros(efields.shape[1:], efields.dtype)

    def slab_paths(slab):
        def paths(i, c):
            for q in range(BATCH // 2):
                first = BATCH * i + 2 * q
                pair = [whole[slab, pl.ds((first + b) * count, count)].reshape(count * GROUP, LANES) for b in range(2)]
                diff = jnp.dot(mix[...], jnp.concatenate(pair, axis=1), preferred_element_type=jnp.float32)
                for b in range(2):
                    path[:, first + b] = diff[:, b * LANES : (b + 1) * LANES].reshape(fields, GROUP, LANES)
            return c

        batches = 0
        for number, tiles in enumerate(layout):
            batches = jnp.where(slab == number, -(-len(tiles) // BATCH), batches)
        lax.fori_loop(0, batches, paths, 0)

    def fill(field, tiles, f, inv):
        for t, (group, columns) in enumerate(tiles):
            r = group * GROUP
            cosine, sine = rounded_sincos(path[f, t] * inv)
            for c in columns:
                lanes = slice(c * LANES, (c + 1) * LANES)
                hole = opening[r : r + GROUP, lanes]
                efields[field, r : r + GROUP, lanes] = cosine * hole
                efields[field, rows + r : rows + r + GROUP, lanes] = sine * hole

    def inverse_tile(wave):
        inv = inverse[wave]
        return jnp.concatenate([inv[:, :LANES], inv[:, :LANES]], axis=0)

    def accumulate(kernel, field, wave, f):
        part_sum = jnp.dot(kernel, efields[field], preferred_element_type=jnp.float32)
        here = pl.ds(f * upix, upix)
        image[wave, here, :PUP] += part_sum[:upix]
        image[wave, here, PUP:] += part_sum[upix:]

    def handle(event):
        stage, o, c = event
        if stage == 0 and kept_tables:
            def make(l, carry):
                second_table(l, l)
                return carry

            lax.fori_loop(0, waves, make, 0)
        if stage == 1:
            first_landed(o, c).wait_recv()
            for e in range(1, 3 if relay else chips):
                plane_copy(o, c, e).start()
            if o + 1 < slabs:
                first_copy(o + 1, c).start()
        if stage == 2 and relay:
            plane_landed(o, c, 1).wait_recv()
            plane_copy(o, c, 3).start()
        if stage == 3:
            for e in range(2 if relay else 1, chips):
                plane_landed(o, c, e).wait_recv()
            core_copy(o, c, core).start()
        if stage == 4:
            for each in range(CHUNKS):
                core_copy(o, each, 1 - core).wait_recv()

    plan = scheduled_events(slabs, waves)
    last_step = (slabs - 1) * waves

    def step_body(step, carry):
        order = step // waves
        wave = step % waves
        slab = from_slab(order)

        for at, events in plan.items():
            if at < last_step:

                @pl.when(step == at)
                def _():
                    for event in events:
                        handle(event)

        @pl.when(wave == 0)
        def _():
            slab_paths(slab)
            open_slab(slab)

        kernel = x_table(slab, wave)
        inv = inverse_tile(wave)

        def units(tiles):
            for f in range(fields):
                fill(f, tiles, f, inv)
            for f in range(fields):
                accumulate(kernel, f, wave, f)

        for number, tiles in enumerate(layout):
            pl.when(slab == number)(functools.partial(units, tiles))

        return carry

    lax.fori_loop(0, last_step, step_body, 0)

    last = from_slab(slabs - 1)

    def make_x(l, c):
        xtables[l] = x_table(last, l)
        return c

    lax.fori_loop(0, waves, make_x, 0)
    open_slab(last)
    for event in plan[last_step]:
        handle(event)
    slab_paths(last)

    def sum_copy(f, shift):
        at = (f, shift - 1)
        return remote(total.at[f], arrived.at[shift - 1, f], sum_send.at[at], sum_recv.at[at], wave_peer(shift))

    def exchange(f):
        return remote(power.at[f, 1 - side], incoming.at[f], out_send.at[f], out_recv.at[f], partner)

    def last_units(f):
        def some_waves(i, c):
            def units(tiles):
                for b in range(AHEAD):
                    fill(b, tiles, f, inverse_tile(AHEAD * i + b))
                for b in range(AHEAD):
                    accumulate(xtables[AHEAD * i + b], b, AHEAD * i + b, f)

            for number, tiles in enumerate(layout):
                pl.when(last == number)(functools.partial(units, tiles))
            return c

        lax.fori_loop(0, waves // AHEAD, some_waves, 0)

    def last_images(f):
        here = pl.ds(pl.multiple_of(f * upix, GROUP), upix)

        def finish(i, c):
            for b in range(AHEAD):
                wave = AHEAD * i + b
                if not kept_tables:
                    second_table(wave, 0)
                field = jnp.dot(
                    image[wave, here, :].astype(jnp.bfloat16),
                    tables[wave if kept_tables else 0],
                    preferred_element_type=jnp.float32,
                )
                re, im = field[:, :PIX], field[:, PIX:]
                bright = re * re + im * im
                for h in range(2):
                    power[f, h, wave] = bright[h * upix // 2 : (h + 1) * upix // 2].astype(jnp.bfloat16)
                total[f, pl.ds(wave, 1), :] = jnp.sum(bright, axis=0, keepdims=True)
            return c

        lax.fori_loop(0, waves // AHEAD, finish, 0)
        total[f] = jnp.broadcast_to(jnp.sum(total[f], axis=1, keepdims=True), (waves, PIX))
        for d in range(1, slabs):
            sum_copy(f, d).start()
        exchange(f).start()

    def mix_field(field, everything, source):
        level_all = 1.0 / (everything * (1.0 / (PIX * PIX)) + EPSILON)
        levels = [level_all[l : l + 1, :] for l in range(waves)]
        step = 16

        def chunk(i, c):
            r = pl.multiple_of(i * step, step)
            sums = [None] * templates
            for l in range(waves):
                spectrum = source[l, pl.ds(r, step), :].astype(jnp.float32) * levels[l]
                for j in range(templates):
                    term = spectrum * weights[pl.ds(field * templates + j, 1), l * PIX : (l + 1) * PIX]
                    sums[j] = term if l == 0 else sums[j] + term
            for j in range(templates):
                mixed[field, j, pl.ds(r, step), :] = sums[j].astype(jnp.bfloat16)
            return c

        lax.fori_loop(0, upix // 2 // step, chunk, 0)
        result_copy(field).start()

    def result_copy(field):
        return pltpu.make_async_copy(mixed.at[field], out_ref.at[field], result_sem.at[field])

    def mix_own(f):
        everything = total[f]
        for d in range(2, slabs, 2):
            sum_copy(f, d).wait()
            everything = everything + arrived[d - 1, f]
        mix_field(side * fields + f, everything, power.at[f, side])

    def mix_other(f):
        everything = None
        for d in range(1, slabs, 2):
            sum_copy(f, d).wait()
            everything = arrived[d - 1, f] if d == 1 else everything + arrived[d - 1, f]
        exchange(f).wait()
        mix_field((1 - side) * fields + f, everything, incoming.at[f])

    def tail(f, carry):
        last_units(f)

        @pl.when(f > 0)
        def _():
            mix_own(f - 1)

        @pl.when(f > 1)
        def _():
            mix_other(f - 2)

        last_images(f)
        return carry

    lax.fori_loop(0, fields, tail, 0)
    mix_own(fields - 1)
    for f in range(max(fields - 2, 0), fields):
        mix_other(f)

    for field in range(2 * fields):
        result_copy(field).wait()
    for d in range(1, slabs):
        length_copy(d, me).wait_send()
    for o in range(1, slabs):
        for c in range(CHUNKS):
            first_copy(o, c).wait_send()
            for e in range(1, chips):
                plane_copy(o, c, e).wait_send()
            core_copy(o, c, core).wait_send()


def local(sizes, waves, mode_basis, coef_table, table_index, wave_lengths, sed_table, template_ids):
    slabs, field_parts, group_parts = sizes
    count, rows, _ = mode_basis.shape
    fields, templates = template_ids.shape
    upix = 2 * PIX // slabs
    half = fields // 2
    chips = field_parts * group_parts // 2
    tiles = max(len(t) for t in packed_tiles(slabs, rows))
    share = -(-tiles * count // (2 * CHUNKS * chips))
    even = -(-tiles // BATCH) * BATCH
    units = max(share * 2 * CHUNKS * chips, even * count)

    hops = slabs - 1
    dma = pltpu.SemaphoreType.DMA

    return pl.pallas_call(
        functools.partial(psf_kernel, sizes, waves, half, share),
        in_specs=[
            pl.BlockSpec(memory_space=pltpu.VMEM),
            pl.BlockSpec(memory_space=pltpu.VMEM),
            pl.BlockSpec(memory_space=pltpu.SMEM),
            pl.BlockSpec(memory_space=pltpu.SMEM),
            pl.BlockSpec(memory_space=pltpu.SMEM),
            pl.BlockSpec(memory_space=pl.ANY),
        ],
        out_specs=pl.BlockSpec(memory_space=pl.ANY),
        out_shape=jax.ShapeDtypeStruct((fields, templates, upix // 2, PIX), jnp.bfloat16),
        scratch_shapes=[
            pltpu.VMEM((half * GROUP, count * GROUP), jnp.bfloat16),
            pltpu.VMEM((fields * templates, waves * PIX), jnp.float32),
            pltpu.VMEM((count, rows, PUP), jnp.bfloat16),
            pltpu.VMEM((slabs, units, GROUP, LANES), jnp.bfloat16),
            pltpu.VMEM((waves, 8, max(2 * rows, PIX)), jnp.float32),
            pltpu.VMEM((half, even, GROUP, LANES), jnp.float32),
            pltpu.VMEM((waves, half * upix, 2 * PUP), jnp.float32),
            pltpu.VMEM((waves if waves <= 8 else 1, 2 * PUP, 2 * PIX), jnp.bfloat16),
            pltpu.VMEM((waves, 2 * upix, 2 * rows), jnp.bfloat16),
            pltpu.VMEM((max(half, AHEAD), 2 * rows, PUP), jnp.bfloat16),
            pltpu.VMEM((rows, PUP), jnp.bfloat16),
            pltpu.VMEM((half, 2, waves, upix // 2, PIX), jnp.bfloat16),
            pltpu.VMEM((half, waves, PIX), jnp.float32),
            pltpu.VMEM((hops, half, waves, PIX), jnp.float32),
            pltpu.VMEM((half, waves, upix // 2, PIX), jnp.bfloat16),
            pltpu.VMEM((fields, templates, upix // 2, PIX), jnp.bfloat16),
            dma,
            dma((hops,)),
            dma((hops,)),
            dma((hops, CHUNKS)),
            dma((hops, CHUNKS)),
            dma((hops, CHUNKS, chips - 1)),
            dma((hops, CHUNKS, chips - 1)),
            dma((hops, CHUNKS)),
            dma((hops, CHUNKS)),
            dma((half, hops)),
            dma((half, hops)),
            dma((half,)),
            dma((half,)),
            dma((fields,)),
        ],
        compiler_params=pltpu.CompilerParams(
            vmem_limit_bytes=LIMIT * 2**20, collective_id=0, has_side_effects=True
        ),
    )(coef_table.T, sed_table.T, table_index, template_ids, wave_lengths, mode_basis)


def solution(mesh):
    sizes = (mesh.shape["wave"], mesh.shape["field"], mesh.shape["groups"])


    def whole_program(*args):
        return sharded(mesh, functools.partial(local, sizes, args[3].shape[0]))(*args)

    return whole_program


def sharded(mesh, body):
    return jax.shard_map(
        body,
        mesh=mesh,
        in_specs=(
            P(None, "wave", None),
            P(),
            P(("groups", "field")),
            P("wave"),
            P(),
            P(("groups", "field"), None),
        ),
        out_specs=P(("groups", "field"), None, "wave", None),
        check_vma=False,
    )
```

```python
import functools

import jax
import jax.numpy as jnp
import numpy as np
from jax import lax
from jax.experimental import pallas as pl
from jax.experimental.pallas import tpu as pltpu
from jax.sharding import PartitionSpec as P

PUP = 512
PIX = 256
EPSILON = 1e-06
GROUP = 16
LANES = 128
CHUNKS = 2
AHEAD = 8
BATCH = 6
LIMIT = 54
ROUNDER = 12582912.0

SIN = (4.442879676818848, -7.307816505432129, 3.5977742671966553, -0.7911993861198425)
COS = (1.4142135381698608, -6.978850841522217, 5.739460468292236, -1.883557915687561, 0.3106880187988281)
SHORT_SIN = (4.440917015075684, -7.256804466247559, 3.229630470275879)
SHORT_COS = (1.4140625, -6.96875, 5.65625, -1.7265625)


def horner(coefficients, s):
    value = coefficients[-1]
    for c in coefficients[-2::-1]:
        value = c + s * value
    return value


def turns_sincos(turns, sine=SIN, cosine=COS):
    nearest = (turns + ROUNDER) - ROUNDER
    r = turns - nearest
    s = r * r
    a = r * horner(sine, s)
    b = horner(cosine, s)
    return 1.0 - a * a, a * b


def rounded_sincos(turns):
    nearest = (turns + ROUNDER) - ROUNDER
    r = turns - nearest
    s = r * r
    a = r * horner(SHORT_SIN, s)
    b = horner([jnp.bfloat16(c) for c in SHORT_COS], s.astype(jnp.bfloat16))
    return (1.0 - a * a).astype(jnp.bfloat16), a.astype(jnp.bfloat16) * b


def packed_tiles(slabs, rows):
    pos = 2 * np.arange(PUP) - PUP + 1
    radius = pos[:, None] ** 2 + pos[None, :] ** 2
    inside = (radius <= PUP * PUP) & (radius >= (61 * PUP // 100) ** 2)
    columns = PUP // LANES
    half = LANES // 2
    result = []
    for slab in range(slabs):
        tiles = []
        for group in range(rows // GROUP):
            first = slab * rows + group * GROUP
            need = inside[first : first + GROUP].any(axis=0).reshape(columns, LANES)
            full = inside[first : first + GROUP].all(axis=0).reshape(columns, LANES).all(axis=1)
            low, high = need[:, :half].any(axis=1), need[:, half:].any(axis=1)
            lows = [c for c in range(columns) if low[c] and not high[c]]
            highs = [c for c in range(columns) if high[c] and not low[c]]
            pairs = list(zip(lows, highs))
            for c in range(columns):
                if low[c] and high[c]:
                    tiles.append((group, (c,), bool(full[c])))
            tiles += [(group, pair, False) for pair in pairs]
            tiles += [(group, (c,), False) for c in lows[len(pairs) :] + highs[len(pairs) :]]
        result.append(tuple(tiles))
    return result


def hop(order, slabs):
    odd = order % 2
    return odd * ((order + 1) // 2) + (1 - odd) * (slabs - order // 2)


def scheduled_events(slabs, waves):
    timed = []

    def add(block, eighth, *event):
        timed.append(((block * waves + eighth * waves // 8, eighth != 8, len(timed)), event))

    for o in range(1, slabs):
        if o == 1:
            for eighth, event in ((0, (1, 1, 0)), (1, (1, 1, 1)), (4, (2, 1, 0)), (6, (2, 1, 1)), (7, (3, 1, 0))):
                add(0, eighth, *event)
            if slabs > 2:
                add(0, 7, 1, 2, 0)
            add(0, 8, 3, 1, 1)
            if slabs > 2:
                add(0, 8, 1, 2, 1)
            add(0, 8, 0, 1, 0)
            add(0, 8, 4, 1, 0)
        elif o == 2:
            add(1, 0, 2, 2, 0)
            add(1, 2, 2, 2, 1)
            add(1, 2, 3, 2, 0)
            add(1, 6, 3, 2, 1)
            add(1, 8, 4, 2, 0)
        else:
            add(o - 2, 0, 1, o, 0)
            add(o - 2, 5, 1, o, 1)
            add(o - 2, 6, 2, o, 0)
            add(o - 1, 0, 2, o, 1)
            add(o - 1, 4, 3, o, 0)
            add(o - 1, 4, 3, o, 1)
            add(o - 1, 8, 4, o, 0)
    plan = {}
    for (step, *_), event in sorted(timed):
        plan.setdefault(step, []).append(event)
    return plan


def one_hot(targets, rows, columns):
    row = lax.broadcasted_iota(jnp.int32, (rows, columns), 0)
    wanted = jnp.zeros((rows, columns), jnp.int32)
    for i, target in enumerate(targets):
        wanted = jnp.where(row == i, target, wanted)
    column = lax.broadcasted_iota(jnp.int32, (rows, columns), 1)
    return (column == wanted).astype(jnp.float32).astype(jnp.bfloat16)


def same_place(shape, row_shift, column_shift, row_mask=-1, column_mask=-1):
    row = (lax.broadcasted_iota(jnp.int32, shape, 0) >> row_shift) & row_mask
    column = (lax.broadcasted_iota(jnp.int32, shape, 1) >> column_shift) & column_mask
    return (row == column).astype(jnp.float32)


def last_with_last(a, b):
    return lax.dot_general(a, b, (((1,), (1,)), ((), ())), preferred_element_type=jnp.float32)


def gather_parameters(side, fields, templates, waves, count, coef_ref, sed_ref, index_ref, ids_ref, mix, weights):
    bf16 = jnp.bfloat16
    wanted = one_hot([index_ref[side * fields + f] for f in range(fields)], 8 * -(-fields // 8), coef_ref.shape[1])
    coeffs = last_with_last(wanted, coef_ref[...])[:fields].astype(bf16)
    bits = GROUP.bit_length() - 1
    tall = same_place((fields * GROUP, fields), bits, 0).astype(bf16)
    wide = same_place((count, count * GROUP), 0, bits).astype(bf16)
    spread = jnp.dot(tall, coeffs, preferred_element_type=jnp.float32).astype(bf16)
    spread = jnp.dot(spread, wide, preferred_element_type=jnp.float32)
    mix[...] = (spread * same_place(spread.shape, 0, 0, GROUP - 1, GROUP - 1)).astype(bf16)

    ids = [ids_ref[f, j] for f in range(2 * fields) for j in range(templates)]
    wanted = one_hot(ids, 2 * fields * templates, sed_ref.shape[1])
    table = sed_ref[...]
    high = table.astype(bf16)
    middle = (table - high.astype(jnp.float32)).astype(bf16)
    low = (table - high.astype(jnp.float32) - middle.astype(jnp.float32)).astype(bf16)
    raw = last_with_last(wanted, high) + last_with_last(wanted, middle) + last_with_last(wanted, low)
    shares = (raw / jnp.sum(raw, axis=1, keepdims=True)).astype(bf16)
    bits = PIX.bit_length() - 1
    weights[...] = jnp.dot(shares, same_place((waves, waves * PIX), 0, bits).astype(bf16), preferred_element_type=jnp.float32)


def psf_kernel(
    sizes, waves, fields, share, coef_ref, sed_ref, index_ref, ids_ref, length_ref, basis_ref, out_ref,
    mix, weights, held, whole, inverse, path, image, tables, xtables, efields, opening, power, total, arrived, incoming, mixed,
    local_sem, wl_send, wl_recv, send1, recv1, send2, recv2, send3, recv3, sum_send, sum_recv, out_send, out_recv, result_sem,
):
    slabs, field_parts, group_parts = sizes
    count, rows, _ = basis_ref.shape
    upix = 2 * PIX // slabs
    own_waves = waves // slabs
    x_parts = field_parts // 2
    chips = x_parts * group_parts
    templates = out_ref.shape[1]
    layout = packed_tiles(slabs, rows)
    kept_tables = tables.shape[0] == waves

    me = lax.axis_index("wave")
    part = lax.axis_index("field")
    core = part % 2
    chip = lax.axis_index("groups") * x_parts + part // 2
    side = me % 2
    first_pix = (me // 2) * upix
    partner = {"wave": me + 1 - 2 * side}

    def wave_peer(shift):
        return {"wave": (me + shift) % slabs}

    def chip_device(other):
        return {"groups": other // x_parts, "field": (other % x_parts) * 2 + core}

    sibling = {"field": part + 1 - 2 * core}

    def remote(src, dst, send, recv, device):
        return pltpu.make_async_remote_copy(
            src_ref=src, dst_ref=dst, send_sem=send, recv_sem=recv,
            device_id=device, device_id_type=pl.DeviceIdType.MESH,
        )

    def from_slab(order):
        return (me + 2 * slabs - hop(order, slabs)) % slabs

    def block(slab, of_core, chunk, of_chip, pieces=1):
        first = ((of_core * CHUNKS + chunk) * chips + of_chip) * share
        return whole.at[slab, pl.ds(first, pieces * share)]

    def first_copy(order, chunk):
        ref = block(me, core, chunk, chip)
        at = (order - 1, chunk)
        return remote(ref, ref, send1.at[at], recv1.at[at], wave_peer(hop(order, slabs)))

    def first_landed(order, chunk):
        ref = block(from_slab(order), core, chunk, chip)
        at = (order - 1, chunk)
        return remote(ref, ref, send1.at[at], recv1.at[at], wave_peer(hop(order, slabs)))

    relay = x_parts == 2 and group_parts == 2
    chip_x, chip_y = chip % x_parts, chip // x_parts
    flip_x, flip_y = 1 - 2 * chip_x, 1 - 2 * chip_y
    first_chip = (chip_y + core * flip_y) * x_parts + chip_x + (1 - core) * flip_x
    second_chip = (chip_y + (1 - core) * flip_y) * x_parts + chip_x + core * flip_x

    def plane_copy(order, chunk, shift):
        at = (order - 1, chunk, shift - 1)
        slab = from_slab(order)
        if relay:
            ref = block(slab, core, chunk, first_chip if shift == 3 else chip)
            device = chip_device(first_chip if shift == 1 else second_chip)
        else:
            ref = block(slab, core, chunk, chip)
            device = chip_device((chip + shift) % chips)
        return remote(ref, ref, send2.at[at], recv2.at[at], device)

    def plane_landed(order, chunk, shift):
        at = (order - 1, chunk, shift - 1)
        if relay:
            sender = (first_chip, second_chip, chips - 1 - chip)[shift - 1]
        else:
            sender = (chip + chips - shift) % chips
        ref = block(from_slab(order), core, chunk, sender)
        return remote(ref, ref, send2.at[at], recv2.at[at], chip_device((chip + shift) % chips))

    def core_copy(order, chunk, which):
        ref = block(from_slab(order), which, chunk, 0, chips)
        at = (order - 1, chunk)
        return remote(ref, ref, send3.at[at], recv3.at[at], sibling)

    def length_copy(shift, sender):
        ref = inverse.at[pl.ds(sender * own_waves, own_waves)]
        return remote(ref, ref, wl_send.at[shift - 1], wl_recv.at[shift - 1], wave_peer(shift))

    barrier = pltpu.get_barrier_semaphore()
    peers = [wave_peer(d) for d in range(1, slabs)] + [chip_device((chip + e) % chips) for e in range(1, chips)] + [sibling]
    for peer in peers:
        pl.semaphore_signal(barrier, inc=1, device_id=peer, device_id_type=pl.DeviceIdType.MESH)
    bring = pltpu.make_async_copy(basis_ref, held, local_sem)
    bring.start()
    for i in range(own_waves):
        inverse[me * own_waves + i] = 1.0 / jnp.full(inverse.shape[1:], length_ref[i], jnp.float32)

    def clear(f, carry):
        for l in range(waves):
            image[l, pl.ds(f * upix, upix), :] = jnp.zeros((upix, 2 * PUP), jnp.float32)
        return carry

    bring.wait()

    low_lanes = (lax.broadcasted_iota(jnp.int32, (GROUP, LANES), 1) < LANES // 2).astype(jnp.float32)
    low_lanes, high_lanes = low_lanes.astype(jnp.bfloat16), (1.0 - low_lanes).astype(jnp.bfloat16)

    def pack(tiles, k, carry):
        for t, (group, columns, full) in enumerate(tiles):
            r = group * GROUP
            parts = [held[k, r : r + GROUP, c * LANES : (c + 1) * LANES] for c in columns]
            value = parts[0]
            if len(parts) == 2:
                value = parts[0] * low_lanes + parts[1] * high_lanes
            whole[me, t * count + k] = value
        return carry

    for slab, tiles in enumerate(layout):

        @pl.when(me == slab)
        def _():
            lax.fori_loop(0, count, functools.partial(pack, tiles), 0)

    pl.semaphore_wait(barrier, len(peers))
    for c in range(CHUNKS):
        first_copy(1, c).start()
    for d in range(1, slabs):
        length_copy(d, me).start()
    gather_parameters(side, fields, templates, waves, count, coef_ref, sed_ref, index_ref, ids_ref, mix, weights)
    lax.fori_loop(0, fields, clear, 0)
    for d in range(1, slabs):
        length_copy(d, (me + slabs - d) % slabs).wait_recv()

    def second_table(wave, slot):
        scale = inverse[wave][:1, :PIX] * (0.25 / (2.0 * PUP))
        step = 64
        for r in range(0, PUP, step):
            ys = 2 * (r + lax.broadcasted_iota(jnp.int32, (step, PIX), 0)) - PUP + 1
            vs = lax.broadcasted_iota(jnp.int32, (step, PIX), 1) - PIX // 2
            cosine, sine = turns_sincos((ys * vs).astype(jnp.float32) * scale)
            cosine = cosine.astype(jnp.bfloat16)
            tables[slot, r : r + step, :PIX] = cosine
            tables[slot, r : r + step, PIX:] = (-sine).astype(jnp.bfloat16)
            tables[slot, PUP + r : PUP + r + step, :PIX] = sine.astype(jnp.bfloat16)
            tables[slot, PUP + r : PUP + r + step, PIX:] = cosine

    def x_table(slab, wave):
        xs = 2 * (slab * rows + lax.broadcasted_iota(jnp.int32, (upix, rows), 1)) - PUP + 1
        us = first_pix + lax.broadcasted_iota(jnp.int32, (upix, rows), 0) - PIX // 2
        scale = inverse[wave][:1, :rows] * (0.25 / (2.0 * PUP))
        cosine, sine = turns_sincos((us * xs).astype(jnp.float32) * scale)
        upper = jnp.concatenate([cosine, sine], axis=1)
        lower = jnp.concatenate([-sine, cosine], axis=1)
        return jnp.concatenate([upper, lower], axis=0).astype(jnp.bfloat16)

    def open_slab(slab):
        def openings(g, c):
            r = pl.multiple_of(g * GROUP, GROUP)
            x = 2 * (slab * rows + r + lax.broadcasted_iota(jnp.int32, (GROUP, PUP), 0)) - PUP + 1
            y = 2 * lax.broadcasted_iota(jnp.int32, (GROUP, PUP), 1) - PUP + 1
            radius = x * x + y * y
            inner = 61 * PUP // 100
            inside = (radius <= PUP * PUP) & (radius >= inner * inner)
            opening[pl.ds(r, GROUP), :] = inside.astype(jnp.float32).astype(jnp.bfloat16)
            return c

        lax.fori_loop(0, rows // GROUP, openings, 0)
        for i in range(efields.shape[0]):
            efields[i] = jnp.zeros(efields.shape[1:], efields.dtype)

    def slab_paths(slab):
        def paths(i, c):
            for q in range(BATCH // 2):
                first = BATCH * i + 2 * q
                pair = [whole[slab, pl.ds((first + b) * count, count)].reshape(count * GROUP, LANES) for b in range(2)]
                diff = jnp.dot(mix[...], jnp.concatenate(pair, axis=1), preferred_element_type=jnp.float32)
                for b in range(2):
                    path[:, first + b] = diff[:, b * LANES : (b + 1) * LANES].reshape(fields, GROUP, LANES)
            return c

        batches = 0
        for number, tiles in enumerate(layout):
            batches = jnp.where(slab == number, -(-len(tiles) // BATCH), batches)
        lax.fori_loop(0, batches, paths, 0)

    def fill(field, tiles, f, inv):
        for t, (group, columns, full) in enumerate(tiles):
            r = group * GROUP
            cosine, sine = rounded_sincos(path[f, t] * inv)
            for c in columns:
                lanes = slice(c * LANES, (c + 1) * LANES)
                hole = None if full else opening[r : r + GROUP, lanes]
                efields[field, r : r + GROUP, lanes] = cosine if full else cosine * hole
                efields[field, rows + r : rows + r + GROUP, lanes] = sine if full else sine * hole

    def inverse_tile(wave):
        inv = inverse[wave]
        return jnp.concatenate([inv[:, :LANES], inv[:, :LANES]], axis=0)

    def accumulate(kernel, field, wave, f):
        part_sum = jnp.dot(kernel, efields[field], preferred_element_type=jnp.float32)
        here = pl.ds(f * upix, upix)
        image[wave, here, :PUP] += part_sum[:upix]
        image[wave, here, PUP:] += part_sum[upix:]

    def handle(event):
        stage, o, c = event
        if stage == 0 and kept_tables:
            def make(l, carry):
                second_table(l, l)
                return carry

            lax.fori_loop(0, waves, make, 0)
        if stage == 1:
            first_landed(o, c).wait_recv()
            for e in range(1, 3 if relay else chips):
                plane_copy(o, c, e).start()
            if o + 1 < slabs:
                first_copy(o + 1, c).start()
        if stage == 2 and relay:
            plane_landed(o, c, 1).wait_recv()
            plane_copy(o, c, 3).start()
        if stage == 3:
            for e in range(2 if relay else 1, chips):
                plane_landed(o, c, e).wait_recv()
            core_copy(o, c, core).start()
        if stage == 4:
            for each in range(CHUNKS):
                core_copy(o, each, 1 - core).wait_recv()

    plan = scheduled_events(slabs, waves)
    last_step = (slabs - 1) * waves

    def step_body(step, carry):
        order = step // waves
        wave = step % waves
        slab = from_slab(order)

        for at, events in plan.items():
            if at < last_step:

                @pl.when(step == at)
                def _():
                    for event in events:
                        handle(event)

        @pl.when(wave == 0)
        def _():
            slab_paths(slab)
            open_slab(slab)

        kernel = x_table(slab, wave)
        inv = inverse_tile(wave)

        def units(tiles):
            for f in range(fields):
                fill(f, tiles, f, inv)
            for f in range(fields):
                accumulate(kernel, f, wave, f)

        for number, tiles in enumerate(layout):
            pl.when(slab == number)(functools.partial(units, tiles))

        return carry

    lax.fori_loop(0, last_step, step_body, 0)

    last = from_slab(slabs - 1)

    def make_x(l, c):
        xtables[l] = x_table(last, l)
        return c

    lax.fori_loop(0, waves, make_x, 0)
    open_slab(last)
    for event in plan[last_step]:
        handle(event)
    slab_paths(last)

    def sum_copy(f, shift):
        at = (f, shift - 1)
        return remote(total.at[f], arrived.at[shift - 1, f], sum_send.at[at], sum_recv.at[at], wave_peer(shift))

    def exchange(f):
        return remote(power.at[f, 1 - side], incoming.at[f], out_send.at[f], out_recv.at[f], partner)

    def last_units(f):
        def some_waves(i, c):
            def units(tiles):
                for b in range(AHEAD):
                    fill(b, tiles, f, inverse_tile(AHEAD * i + b))
                for b in range(AHEAD):
                    accumulate(xtables[AHEAD * i + b], b, AHEAD * i + b, f)

            for number, tiles in enumerate(layout):
                pl.when(last == number)(functools.partial(units, tiles))
            return c

        lax.fori_loop(0, waves // AHEAD, some_waves, 0)

    def last_images(f):
        here = pl.ds(pl.multiple_of(f * upix, GROUP), upix)

        def finish(i, c):
            for b in range(AHEAD):
                wave = AHEAD * i + b
                if not kept_tables:
                    second_table(wave, 0)
                field = jnp.dot(
                    image[wave, here, :].astype(jnp.bfloat16),
                    tables[wave if kept_tables else 0],
                    preferred_element_type=jnp.float32,
                )
                re, im = field[:, :PIX], field[:, PIX:]
                bright = re * re + im * im
                for h in range(2):
                    power[f, h, wave] = bright[h * upix // 2 : (h + 1) * upix // 2].astype(jnp.bfloat16)
                total[f, pl.ds(wave, 1), :] = jnp.sum(bright, axis=0, keepdims=True)
            return c

        lax.fori_loop(0, waves // AHEAD, finish, 0)
        total[f] = jnp.broadcast_to(jnp.sum(total[f], axis=1, keepdims=True), (waves, PIX))
        for d in range(1, slabs):
            sum_copy(f, d).start()
        exchange(f).start()

    def mix_field(field, everything, source):
        level_all = 1.0 / (everything * (1.0 / (PIX * PIX)) + EPSILON)
        levels = [level_all[l : l + 1, :] for l in range(waves)]
        step = 16

        def chunk(i, c):
            r = pl.multiple_of(i * step, step)
            sums = [None] * templates
            for l in range(waves):
                spectrum = source[l, pl.ds(r, step), :].astype(jnp.float32) * levels[l]
                for j in range(templates):
                    term = spectrum * weights[pl.ds(field * templates + j, 1), l * PIX : (l + 1) * PIX]
                    sums[j] = term if l == 0 else sums[j] + term
            for j in range(templates):
                mixed[field, j, pl.ds(r, step), :] = sums[j].astype(jnp.bfloat16)
            return c

        lax.fori_loop(0, upix // 2 // step, chunk, 0)
        result_copy(field).start()

    def result_copy(field):
        return pltpu.make_async_copy(mixed.at[field], out_ref.at[field], result_sem.at[field])

    def mix_own(f):
        everything = total[f]
        for d in range(2, slabs, 2):
            sum_copy(f, d).wait()
            everything = everything + arrived[d - 1, f]
        mix_field(side * fields + f, everything, power.at[f, side])

    def mix_other(f):
        everything = None
        for d in range(1, slabs, 2):
            sum_copy(f, d).wait()
            everything = arrived[d - 1, f] if d == 1 else everything + arrived[d - 1, f]
        exchange(f).wait()
        mix_field((1 - side) * fields + f, everything, incoming.at[f])

    def tail(f, carry):
        last_units(f)

        @pl.when(f > 0)
        def _():
            mix_own(f - 1)

        @pl.when(f > 1)
        def _():
            mix_other(f - 2)

        last_images(f)
        return carry

    lax.fori_loop(0, fields, tail, 0)
    mix_own(fields - 1)
    for f in range(max(fields - 2, 0), fields):
        mix_other(f)

    for field in range(2 * fields):
        result_copy(field).wait()
    for d in range(1, slabs):
        length_copy(d, me).wait_send()
    for o in range(1, slabs):
        for c in range(CHUNKS):
            first_copy(o, c).wait_send()
            for e in range(1, chips):
                plane_copy(o, c, e).wait_send()
            core_copy(o, c, core).wait_send()


def local(sizes, waves, mode_basis, coef_table, table_index, wave_lengths, sed_table, template_ids):
    slabs, field_parts, group_parts = sizes
    count, rows, _ = mode_basis.shape
    fields, templates = template_ids.shape
    upix = 2 * PIX // slabs
    half = fields // 2
    chips = field_parts * group_parts // 2
    tiles = max(len(t) for t in packed_tiles(slabs, rows))
    share = -(-tiles * count // (2 * CHUNKS * chips))
    even = -(-tiles // BATCH) * BATCH
    units = max(share * 2 * CHUNKS * chips, even * count)

    hops = slabs - 1
    dma = pltpu.SemaphoreType.DMA

    return pl.pallas_call(
        functools.partial(psf_kernel, sizes, waves, half, share),
        in_specs=[
            pl.BlockSpec(memory_space=pltpu.VMEM),
            pl.BlockSpec(memory_space=pltpu.VMEM),
            pl.BlockSpec(memory_space=pltpu.SMEM),
            pl.BlockSpec(memory_space=pltpu.SMEM),
            pl.BlockSpec(memory_space=pltpu.SMEM),
            pl.BlockSpec(memory_space=pl.ANY),
        ],
        out_specs=pl.BlockSpec(memory_space=pl.ANY),
        out_shape=jax.ShapeDtypeStruct((fields, templates, upix // 2, PIX), jnp.bfloat16),
        scratch_shapes=[
            pltpu.VMEM((half * GROUP, count * GROUP), jnp.bfloat16),
            pltpu.VMEM((fields * templates, waves * PIX), jnp.float32),
            pltpu.VMEM((count, rows, PUP), jnp.bfloat16),
            pltpu.VMEM((slabs, units, GROUP, LANES), jnp.bfloat16),
            pltpu.VMEM((waves, 8, max(2 * rows, PIX)), jnp.float32),
            pltpu.VMEM((half, even, GROUP, LANES), jnp.float32),
            pltpu.VMEM((waves, half * upix, 2 * PUP), jnp.float32),
            pltpu.VMEM((waves if waves <= 8 else 1, 2 * PUP, 2 * PIX), jnp.bfloat16),
            pltpu.VMEM((waves, 2 * upix, 2 * rows), jnp.bfloat16),
            pltpu.VMEM((max(half, AHEAD), 2 * rows, PUP), jnp.bfloat16),
            pltpu.VMEM((rows, PUP), jnp.bfloat16),
            pltpu.VMEM((half, 2, waves, upix // 2, PIX), jnp.bfloat16),
            pltpu.VMEM((half, waves, PIX), jnp.float32),
            pltpu.VMEM((hops, half, waves, PIX), jnp.float32),
            pltpu.VMEM((half, waves, upix // 2, PIX), jnp.bfloat16),
            pltpu.VMEM((fields, templates, upix // 2, PIX), jnp.bfloat16),
            dma,
            dma((hops,)),
            dma((hops,)),
            dma((hops, CHUNKS)),
            dma((hops, CHUNKS)),
            dma((hops, CHUNKS, chips - 1)),
            dma((hops, CHUNKS, chips - 1)),
            dma((hops, CHUNKS)),
            dma((hops, CHUNKS)),
            dma((half, hops)),
            dma((half, hops)),
            dma((half,)),
            dma((half,)),
            dma((fields,)),
        ],
        compiler_params=pltpu.CompilerParams(
            vmem_limit_bytes=LIMIT * 2**20, collective_id=0, has_side_effects=True
        ),
    )(coef_table.T, sed_table.T, table_index, template_ids, wave_lengths, mode_basis)


def solution(mesh):
    sizes = (mesh.shape["wave"], mesh.shape["field"], mesh.shape["groups"])


    def whole_program(*args):
        return sharded(mesh, functools.partial(local, sizes, args[3].shape[0]))(*args)

    return whole_program


def sharded(mesh, body):
    return jax.shard_map(
        body,
        mesh=mesh,
        in_specs=(
            P(None, "wave", None),
            P(),
            P(("groups", "field")),
            P("wave"),
            P(),
            P(("groups", "field"), None),
        ),
        out_specs=P(("groups", "field"), None, "wave", None),
        check_vma=False,
    )
```
